128 devices in a mesh: band: 8 (over z, core), sector: 16 (over x, y).
Axes of the slice: x: 4, y: 4, z: 4, core: 2. Of those that a mesh axis runs over, the one named last changes fastest.
Arguments:
- base_state: float32 [128, 256, 1536], P('band', 'sector'), may hold values from -6 to 6
- direction: float32 [128, 256, 1536], P('band', 'sector'), may hold values from -24 to 24
- residual: float32 [128, 256, 1536], P('band', 'sector'), may hold values from -24 to 24
- mix_coef: float32 [9, 1536], replicated, may hold values from -2.5 to 2.5
- w_in: bfloat16 [1536, 3072], replicated, may hold values from -0.15625 to 0.15625
- w_out: bfloat16 [3072, 1536], replicated, may hold values from -0.109375 to 0.109375
- obs_patch: int32 [128, 128, 4], P(('band', 'sector')), may hold values from 0 to 255
- obs_count: int32 [128, 128], P(('band', 'sector')), may hold values from 0 to 4, as said below
- obs_pos: int32 [128, 128, 4, 4], P(('band', 'sector')), may hold values from 0 to 1535
- obs_wgt: float32 [128, 128, 4, 4], P(('band', 'sector')), may hold values from 0.2 to 1
- obs_rinv: float32 [128, 128, 4], P(('band', 'sector')), may hold values from 1 to 1500
Outputs:
- next_residual: float32 [128, 256, 1536], P('band', 'sector')
The draws below stay inside these ranges and needn't reach their ends.
Inputs may be any that keep to these rules, and one draw needn't show every extreme that they name: `obs_count`: live station slots of one owner for one source block are that pair's first slots; in every draw some source block has all 4 slots live from every owner.
All inputs are finite; a program needn't handle non-finite values.
Results may differ from the reference program's by a relative error of at most 0.006.
Values may be sent and summed in bfloat16 or wider, within the bound.
A program may use at most 128 MiB of HBM per device.

```python
import math
import jax
import jax.numpy as jnp
from jax import lax

D = 1536
FF = 3072
LAT_DEV = 16
LON_DEV = 16
CAP = 4
TAPS = 4
NLAT = 128
NLON = 256
OWNERS = 128
N_BAND = 8
N_SECTOR = 16


def ladder(key, entries, spread):
    ordering = jax.random.permutation(key, entries).astype(jnp.float32)
    return jnp.exp(ordering / (entries - 1) * math.log(spread))


def rough_field(key, noise, row_span, sector_span):
    row_scale = jnp.exp(jax.random.uniform(jax.random.fold_in(key, 5), (NLAT, NLON, 1), jnp.float32) * math.log(row_span)) / math.sqrt(row_span)
    col_scale = jnp.exp(jax.random.uniform(jax.random.fold_in(key, 6), (1, 1, D), jnp.float32) * math.log(10.0)) / math.sqrt(10.0)
    growth = jnp.exp(jnp.arange(NLAT, dtype=jnp.float32)[:, None, None] / NLAT * math.log(3.0)) / math.sqrt(3.0)
    sector_amp = ladder(jax.random.fold_in(key, 7), N_SECTOR, sector_span) / math.sqrt(sector_span)
    column_amp = jnp.repeat(sector_amp, LON_DEV)[None, :, None]
    return jnp.clip(noise * row_scale * col_scale * growth * column_amp, -24.0, 24.0)


def draw_direction(key, part):
    key = jax.random.fold_in(key, 21)
    noise = jax.random.normal(jax.random.fold_in(key, 1), (NLAT, NLON, D), jnp.float32)
    return rough_field(key, noise, 10.0, 4.0)


def draw_residual(key, part):
    key = jax.random.fold_in(key, 37)
    noise = jax.random.normal(jax.random.fold_in(key, 1), (NLAT, NLON, D), jnp.float32)
    return rough_field(key, noise, 10.0, 1.0)


def draw_obs_count(key, part):
    key = jax.random.fold_in(key, 11)
    crowded = jax.random.randint(jax.random.fold_in(key, 1), (1, OWNERS), 0, 2)
    many_obs = jax.random.randint(jax.random.fold_in(key, 2), (OWNERS, OWNERS), CAP - 1, CAP + 1)
    few_obs = jax.random.randint(jax.random.fold_in(key, 3), (OWNERS, OWNERS), 0, CAP // 2 + 1)
    counts = jnp.where(crowded == 1, many_obs, few_obs)
    filled = jax.random.randint(jax.random.fold_in(key, 4), (), 0, OWNERS)
    counts = jnp.where(jnp.arange(OWNERS, dtype=jnp.int32)[None, :] == filled, CAP, counts)
    return counts.astype(jnp.int32)


def draw_obs_rinv(key, part):
    key = jax.random.fold_in(key, 43)
    owner_ids = jnp.arange(OWNERS, dtype=jnp.int32)
    own_band = owner_ids // N_SECTOR
    own_sector = owner_ids % N_SECTOR
    owner_factor = ladder(jax.random.fold_in(key, 1), N_SECTOR, 6.0)[own_sector] * ladder(jax.random.fold_in(key, 2), N_BAND, 3.0)[own_band]
    block_factor = ladder(jax.random.fold_in(key, 3), N_BAND, 3.0)[own_band] * ladder(jax.random.fold_in(key, 4), N_SECTOR, 3.0)[own_sector]
    nearby = jnp.where(own_sector[:, None] == own_sector[None, :], 16.0, 1.0)
    base_scale = jnp.exp(jax.random.uniform(jax.random.fold_in(key, 5), (OWNERS, OWNERS, CAP), jnp.float32) * math.log(2.0))
    combined = base_scale * owner_factor[:, None, None] * block_factor[None, :, None] * nearby[:, :, None]
    return jnp.minimum(combined, 1500.0)


def with_ends(values, own_key, low, largest):
    extent = values.shape
    spot = [jax.random.randint(jax.random.fold_in(own_key, axis), (), 0, extent[axis]) for axis in range(len(extent))]
    values = values.at[tuple(spot)].set(low)
    longest = extent.index(max(extent))
    spot[longest] = (spot[longest] + 1) % extent[longest]
    return values.at[tuple(spot)].set(largest)


def shard_levels(rng, extent, pieces, low, top_value):
    factor_of, own = 1.0, jax.random.fold_in(rng, 6)
    for axis_at, parts in pieces:
        heights = jnp.exp(jax.random.uniform(jax.random.fold_in(own, axis_at), (parts,), jnp.float32, low / len(pieces), top_value / len(pieces)))
        factor_of = factor_of * jnp.repeat(heights, extent[axis_at] // parts).reshape([-1 if axis == axis_at else 1 for axis in range(len(extent))])
    return factor_of


def normal_values(key, dims, scale, most, shards=(), kind=jnp.bfloat16):
    values = jax.random.normal(key, dims, jnp.float32) * scale
    if len(shards) > 0:
        values = shard_levels(key, dims, shards, -0.22, 0.18) * values
    return jnp.clip(values, min=-most, max=most).astype(kind)


def setup_inputs(seed: int = 0) -> dict:
    streams_of = jax.random.split(jax.random.key(seed), 12)
    base_state = normal_values(streams_of[0], (NLAT, NLON, D), 1.0, 6.0, ((0, 8), (1, 16)), jnp.float32)
    direction = draw_direction(jax.random.fold_in(streams_of[11], 71), 0)
    residual = draw_residual(jax.random.fold_in(streams_of[11], 71), 0)
    mix_coef = normal_values(streams_of[3], (9, D), 0.4, 2.5, (), jnp.float32)
    w_in = normal_values(streams_of[4], (D, FF), D ** -0.5, 0.15625)
    w_out = normal_values(streams_of[5], (FF, D), FF ** -0.5, 0.109375)
    obs_patch = with_ends(jax.random.randint(streams_of[6], (OWNERS, OWNERS, CAP), 0, LAT_DEV * LON_DEV), jax.random.fold_in(streams_of[6], 1), 0, (LAT_DEV * LON_DEV) - 1).astype(jnp.int32)
    obs_count = draw_obs_count(jax.random.fold_in(streams_of[11], 71), 0)
    obs_pos = with_ends(jax.random.randint(streams_of[8], (OWNERS, OWNERS, CAP, TAPS), 0, D), jax.random.fold_in(streams_of[8], 1), 0, D - 1).astype(jnp.int32)
    obs_wgt = jnp.clip(0.2 + 0.8 * jax.random.uniform(streams_of[9], (OWNERS, OWNERS, CAP, TAPS), jnp.float32) ** shard_levels(streams_of[9], (OWNERS, OWNERS, CAP, TAPS), ((0, 128),), -0.2, 0.2), 0.2, 1.0)
    obs_rinv = draw_obs_rinv(jax.random.fold_in(streams_of[11], 71), 0)
    return dict(base_state=base_state, direction=direction, residual=residual, mix_coef=mix_coef, w_in=w_in, w_out=w_out, obs_patch=obs_patch, obs_count=obs_count, obs_pos=obs_pos, obs_wgt=obs_wgt, obs_rinv=obs_rinv)


def gelu_slope(preact):
    normal_cdf = 0.5 * (1.0 + jax.scipy.special.erf(preact * (1.0 / math.sqrt(2.0))))
    normal_pdf = jnp.exp(-0.5 * preact * preact) * (1.0 / math.sqrt(2.0 * math.pi))
    return normal_cdf + preact * normal_pdf

def pad_grid(grid_field):
    lon_wide = jnp.concatenate([grid_field[:, -1:], grid_field, grid_field[:, :1]], axis=1)
    return jnp.pad(lon_wide, ((1, 1), (0, 0), (0, 0)))

def stencil_apply(padded, mix_coef, lat_n, lon_n):
    summed = jnp.zeros((lat_n, lon_n, mix_coef.shape[1]), jnp.float32)
    for row_off in range(3):
        for col_off in range(3):
            summed = summed + mix_coef[3 * row_off + col_off] * padded[row_off:row_off + lat_n, col_off:col_off + lon_n]
    return summed

def stencil_adjoint(padded, mix_coef, lat_n, lon_n):
    summed = jnp.zeros((lat_n, lon_n, mix_coef.shape[1]), jnp.float32)
    for row_off in range(3):
        for col_off in range(3):
            summed = summed + mix_coef[3 * row_off + col_off] * padded[2 - row_off:2 - row_off + lat_n, 2 - col_off:2 - col_off + lon_n]
    return summed

def to_blocks(grid_field):
    features = grid_field.shape[-1]
    split = grid_field.reshape(N_BAND, LAT_DEV, N_SECTOR, LON_DEV, features)
    return split.transpose(0, 2, 1, 3, 4).reshape(N_BAND * N_SECTOR, LAT_DEV * LON_DEV, features)

def from_blocks(blocked):
    features = blocked.shape[-1]
    split = blocked.reshape(N_BAND, N_SECTOR, LAT_DEV, LON_DEV, features)
    return split.transpose(0, 2, 1, 3, 4).reshape(N_BAND * LAT_DEV, N_SECTOR * LON_DEV, features)

def reference(base_state, direction, residual, mix_coef, w_in, w_out, obs_patch, obs_count, obs_pos, obs_wgt, obs_rinv):
    lat_n, lon_n, features = base_state.shape
    tok_n = lat_n * lon_n
    mix_base = stencil_apply(pad_grid(base_state), mix_coef, lat_n, lon_n).astype(jnp.bfloat16).reshape(tok_n, features)
    preact = jnp.dot(mix_base, w_in, preferred_element_type=jnp.float32)
    slopes = gelu_slope(preact)
    tangent_mix = stencil_apply(pad_grid(direction), mix_coef, lat_n, lon_n).astype(jnp.bfloat16).reshape(tok_n, features)
    tangent_hidden = (slopes * jnp.dot(tangent_mix, w_in, preferred_element_type=jnp.float32)).astype(jnp.bfloat16)
    tangent = (direction.reshape(tok_n, features) + jnp.dot(tangent_hidden, w_out, preferred_element_type=jnp.float32)).astype(jnp.bfloat16)
    blocked = to_blocks(tangent.reshape(lat_n, lon_n, features))
    slot_n = obs_patch.shape[2]
    source_ids = jnp.arange(obs_patch.shape[1], dtype=jnp.int32)[None, :, None, None]
    patch_col = obs_patch[..., None]
    sampled = blocked[source_ids, patch_col, obs_pos].astype(jnp.float32)
    active = (jnp.arange(slot_n, dtype=jnp.int32)[None, None, :] < obs_count[:, :, None]).astype(jnp.float32)
    misfit = lax.optimization_barrier(jnp.sum(obs_wgt * sampled, axis=-1))
    deposit = (active * obs_rinv * misfit)[..., None] * obs_wgt
    grad_blocks = jnp.zeros(blocked.shape, jnp.float32).at[source_ids, patch_col, obs_pos].add(deposit)
    obs_grad = from_blocks(grad_blocks).reshape(tok_n, features)
    grad_hidden = jnp.dot(obs_grad.astype(jnp.bfloat16), w_out.T, preferred_element_type=jnp.float32)
    grad_act = (slopes * grad_hidden).astype(jnp.bfloat16)
    grad_mix = jnp.dot(grad_act, w_in.T, preferred_element_type=jnp.float32).reshape(lat_n, lon_n, features)
    hess_vec = direction + obs_grad.reshape(lat_n, lon_n, features) + stencil_adjoint(pad_grid(grad_mix), mix_coef, lat_n, lon_n)
    norm_sq = jnp.sum(residual * residual)
    curvature = jnp.sum(direction * hess_vec)
    return residual - norm_sq / curvature * hess_vec
```

```python
import functools
import math

import jax
import jax.numpy as jnp
from jax import lax
from jax.experimental import pallas as pl
from jax.experimental.pallas import tpu as pltpu
from jax.sharding import PartitionSpec as P

MESH = pl.DeviceIdType.MESH
F32 = jnp.float32
BF16 = jnp.bfloat16
LANES = 128


def gelu_slope(preact):
    normal_cdf = 0.5 * (1.0 + lax.erf(preact * (1.0 / math.sqrt(2.0))))
    normal_pdf = jnp.exp(-0.5 * preact * preact) * (1.0 / math.sqrt(2.0 * math.pi))
    return normal_cdf + preact * normal_pdf


def nn(left, right):
    return jnp.dot(left, right, preferred_element_type=F32)


def nt(left, right):
    return lax.dot_general(left, right, (((1,), (1,)), ((), ())), preferred_element_type=F32)


def tn(left, right):
    return lax.dot_general(left, right, (((0,), (0,)), ((), ())), preferred_element_type=F32)


def fold_lanes(values):
    total = values[:, :LANES]
    for at in range(LANES, values.shape[1], LANES):
        total = total + values[:, at : at + LANES]
    return total


def stencil_rows(row, west, east, corners, coef, lat_n, lon_n):
    width = west.shape[1]
    lat_at = lax.broadcasted_iota(jnp.int32, (lat_n, width), 0)
    lon_at = lax.broadcasted_iota(jnp.int32, (lon_n, width), 0)

    def column(mid, above, below, b):
        prev = jnp.where(lat_at == 0, above, pltpu.roll(mid, 1, 0))
        following = jnp.where(lat_at == lat_n - 1, below, pltpu.roll(mid, lat_n - 1, 0))
        return coef[b] * prev + coef[3 + b] * mid + coef[6 + b] * following

    rim_w = column(west, corners[0], corners[2], 0)
    rim_e = column(east, corners[1], corners[3], 2)
    rows = [row(-1), row(0)]
    for i in range(lat_n):
        rows.append(row(i + 1))
        part = [
            coef[b] * rows[i] + coef[3 + b] * rows[i + 1] + coef[6 + b] * rows[i + 2]
            for b in range(3)
        ]
        low = jnp.where(lon_at == 0, rim_w[i : i + 1], pltpu.roll(part[0], 1, 0))
        high = jnp.where(lon_at == lon_n - 1, rim_e[i : i + 1], pltpu.roll(part[2], lon_n - 1, 0))
        yield low + part[1] + high


def kernel(
    sizes,
    base_h, dir_h, res_h, coef_h, win_h, wout_h, patch_h, count_h, pos_h, wgt_h, rinv_h,
    out_ref,
    base, direc, res, coef, win, wout, patch, count, pos, wgt, rinv,
    mixed, slopes, hidden, tang, weights, onehot, spread, obs, obs_b, gmix,
    fedge_s, fedge_r, fcorn_s, fcorn_r, bedge_s, bedge_r, bcorn_s, bcorn_r,
    pay, a0, a1, a2, a3, red0, red1, red2,
    load_sem, win_sem, wout_sem,
    fs_sem, fr_sem, bs_sem, br_sem,
    p1s_sem, p1r_sem, p2s_sem, p2r_sem, r1s_sem, r1r_sem, r2s_sem, r2r_sem,
):
    nb, ns, lat_n, lon_n, feat, hid, slot_n, tap_n, n1, n2, nbk = sizes
    tok_n = lat_n * lon_n
    block_n = nb * ns
    b = lax.axis_index("band")
    s = lax.axis_index("sector")

    def band(step):
        return lax.rem(b + step + nb, nb)

    def sector(step):
        return lax.rem(s + step + ns, ns)

    loads = {}
    pairs = dict(
        patch=(patch_h, patch), count=(count_h, count), pos=(pos_h, pos), wgt=(wgt_h, wgt),
        rinv=(rinv_h, rinv), coef=(coef_h, coef), dir=(dir_h, direc), base=(base_h, base),
    )
    for at, (name, (src, dst)) in enumerate(pairs.items()):
        loads[name] = pltpu.make_async_copy(src, dst, load_sem.at[at])
        loads[name].start()
    win_loads = []
    for at in range(hid // n1):
        cols = pl.ds(at * n1, n1)
        win_loads.append(pltpu.make_async_copy(win_h.at[:, cols], win.at[:, cols], win_sem.at[at]))
        win_loads[-1].start()
    loads["res"] = pltpu.make_async_copy(res_h, res, load_sem.at[8])
    loads["res"].start()
    wout_loads = []
    for at in range(feat // n2):
        cols = pl.ds(at * n2, n2)
        wout_loads.append(pltpu.make_async_copy(wout_h.at[:, cols], wout.at[:, cols], wout_sem.at[at]))
        wout_loads[-1].start()

    diagonal = [(band(db), sector(ds)) for db in (1, -1) for ds in (1, -1)]
    partners = [(band(d), s) for d in range(1, nb)] + [(b, sector(d)) for d in range(1, ns)] + diagonal
    barrier = pltpu.get_barrier_semaphore()
    for partner in partners:
        pl.semaphore_signal(barrier, inc=1, device_id=partner, device_id_type=MESH)

    def send(src, dst, send_sem, recv_sem, to):
        copy = pltpu.make_async_remote_copy(
            src_ref=src, dst_ref=dst, send_sem=send_sem, recv_sem=recv_sem,
            device_id=to, device_id_type=MESH,
        )
        return copy

    edge_to = [(band(1), s), (band(-1), s), (b, sector(1)), (b, sector(-1))]
    corner_to = [
        (band(1), sector(1)), (band(1), sector(-1)), (band(-1), sector(1)), (band(-1), sector(-1)),
    ]
    last_i, last_j = lat_n - 1, lon_n - 1

    for name in ("dir", "base"):
        loads[name].wait()
    for at, field in enumerate((base, direc)):
        for side, rim in enumerate((field[last_i], field[0], field[:, last_j], field[:, 0])):
            fedge_s[side, at] = rim.astype(BF16)
        for side, (ci, cj) in enumerate(((last_i, last_j), (last_i, 0), (0, last_j), (0, 0))):
            fcorn_s[side, at : at + 1] = field[ci, cj : cj + 1]
    pl.semaphore_wait(barrier, len(partners))
    fwd = []
    for side in range(4):
        fwd.append(send(fedge_s.at[side], fedge_r.at[side], fs_sem.at[side], fr_sem.at[side], edge_to[side]))
        fwd[-1].start()
    for side in range(4):
        fwd.append(
            send(fcorn_s.at[side], fcorn_r.at[side], fs_sem.at[4 + side], fr_sem.at[4 + side], corner_to[side])
        )
        fwd[-1].start()

    for name in ("patch", "count", "pos", "wgt", "rinv"):
        loads[name].wait()
    slot_at = lax.broadcasted_iota(jnp.int32, (slot_n, block_n), 0)
    tap_all = slot_n * tap_n
    pay[...] = jnp.zeros_like(pay)
    pay[0:slot_n] = patch[...].astype(F32)
    pay[slot_n : 2 * slot_n] = jnp.where(slot_at < count[...], rinv[...], 0.0)
    pay[2 * slot_n : 2 * slot_n + tap_all] = pos[...].astype(F32)
    pay[2 * slot_n + tap_all : 2 * slot_n + 2 * tap_all] = wgt[...]
    a0[...] = jnp.transpose(pay[...]).reshape(nb, ns, LANES)
    a1[b] = a0[b]
    phase1 = []
    for d in range(1, nb):
        phase1.append(send(a0.at[band(d)], a1.at[b], p1s_sem.at[d - 1], p1r_sem.at[d - 1], (band(d), s)))
        phase1[-1].start()

    loads["res"].wait()
    norm = jnp.zeros((lon_n, LANES), F32)
    grow = jnp.zeros((lon_n, LANES), F32)

    def square(i, carry):
        norm, grow = carry
        r, d = res[i], direc[i]
        return norm + fold_lanes(r * r), grow + fold_lanes(d * d)

    norm, grow = lax.fori_loop(0, lat_n, square, (norm, grow))
    red0[0:1] = jnp.sum(norm, axis=0, keepdims=True)
    red0[1:2] = jnp.sum(grow, axis=0, keepdims=True)

    loads["coef"].wait()
    for copy in fwd:
        copy.wait_recv()
    north = (b > 0).astype(F32)
    south = (b < nb - 1).astype(F32)
    cw = 256

    def mix(k, carry):
        cols = pl.ds(pl.multiple_of(k * cw, cw), cw)
        taps = [coef[t : t + 1, cols] for t in range(9)]
        for at, field in enumerate((base, direc)):
            def row(r):
                if r < 0:
                    return fedge_r[0, at, :, cols].astype(F32) * north
                if r == lat_n:
                    return fedge_r[1, at, :, cols].astype(F32) * south
                return field[r, :, cols]

            corners = [
                fcorn_r[side, at : at + 1, cols] * (north if side < 2 else south) for side in range(4)
            ]
            west = fedge_r[2, at, :, cols].astype(F32)
            east = fedge_r[3, at, :, cols].astype(F32)
            for i, summed in enumerate(stencil_rows(row, west, east, corners, taps, lat_n, lon_n)):
                start = at * tok_n + i * lon_n
                mixed[start : start + lon_n, cols] = summed.astype(BF16)
        return carry

    lax.fori_loop(0, feat // cw, mix, 0)

    phase2 = []
    for n in range(hid // n1):
        win_loads[n].wait()
        cols = slice(n * n1, (n + 1) * n1)
        both = nn(mixed[...], win[:, cols])
        slope = gelu_slope(both[:tok_n])
        slopes[:, cols] = slope
        hidden[:, cols] = (slope * both[tok_n:]).astype(BF16)
        if n == 1:
            for copy in phase1:
                copy.wait_recv()
            for q in range(ns):
                a2[q] = a1[:, q, :]
            a3[s] = a2[s]
            for d in range(1, ns):
                phase2.append(
                    send(a2.at[sector(d)], a3.at[s], p2s_sem.at[d - 1], p2r_sem.at[d - 1], (b, sector(d)))
                )
                phase2[-1].start()
        if n == hid // n1 - 2:
            for copy in phase2:
                copy.wait_recv()

    stations = slot_n * block_n
    told = a3[...].reshape(block_n, LANES)
    cell_at = lax.broadcasted_iota(jnp.int32, (block_n, tok_n), 1).astype(F32)
    for c in range(slot_n):
        onehot[c * block_n : (c + 1) * block_n] = jnp.where(told[:, c : c + 1] == cell_at, 1.0, 0.0).astype(BF16)
    rb = min(32, block_n)
    lane_at = lax.broadcasted_iota(jnp.int32, (rb, LANES), 1).astype(F32)
    for c in range(slot_n):
        for r in range(0, block_n, rb):
            rows = told[r : r + rb]
            first = 2 * slot_n + c * tap_n
            chans = [jnp.broadcast_to(rows[:, first + k : first + k + 1], (rb, LANES)) for k in range(tap_n)]
            first += tap_all
            wgts = [jnp.broadcast_to(rows[:, first + k : first + k + 1], (rb, LANES)) for k in range(tap_n)]
            for j in range(feat // LANES):
                here = lane_at + float(j * LANES)
                summed = jnp.where(chans[0] == here, wgts[0], 0.0)
                for k in range(1, tap_n):
                    summed = summed + jnp.where(chans[k] == here, wgts[k], 0.0)
                weights[c * block_n + r : c * block_n + r + rb, j * LANES : (j + 1) * LANES] = summed

    seen = jnp.zeros((stations, LANES), F32)
    for n in range(feat // n2):
        wout_loads[n].wait()
        cols = slice(n * n2, (n + 1) * n2)
        own = direc[:, :, cols].reshape(tok_n, n2)
        tang[:, cols] = (own + nn(hidden[...], wout[:, cols])).astype(BF16)
        sampled = nn(onehot[...], tang[:, cols])
        seen = seen + fold_lanes(sampled * weights[:, cols])
    misfit = jnp.sum(seen, axis=1, keepdims=True)
    inverse = jnp.concatenate([told[:, slot_n + c : slot_n + c + 1] for c in range(slot_n)], axis=0)
    scaled = inverse * misfit
    lane0 = lax.broadcasted_iota(jnp.int32, (1, LANES), 1) == 0
    red0[1:2] = red0[1:2] + jnp.where(lane0, jnp.sum(scaled * misfit, axis=0, keepdims=True), 0.0)

    reduce1 = []
    red1[b] = red0[...]
    for d in range(1, nb):
        reduce1.append(send(red0, red1.at[b], r1s_sem.at[d - 1], r1r_sem.at[d - 1], (band(d), s)))
        reduce1[-1].start()

    for n in range(feat // n2):
        cols = slice(n * n2, (n + 1) * n2)
        deposit = scaled * weights[:, cols]
        rough = deposit.astype(BF16)
        fine = (deposit - rough.astype(F32)).astype(BF16)
        summed = tn(onehot[...], rough) + tn(onehot[...], fine)
        obs[:, cols] = summed
        obs_b[:, cols] = summed.astype(BF16)

    for n in range(hid // n1):
        rows = slice(n * n1, (n + 1) * n1)
        hidden[:, rows] = (slopes[:, rows] * nt(obs_b[...], wout[rows, :])).astype(BF16)

    for copy in reduce1:
        copy.wait_recv()
    total = red1[0]
    for d in range(1, nb):
        total = total + red1[d]
    red0b = red2.at[s]
    red0b[...] = total
    reduce2 = []
    for d in range(1, ns):
        reduce2.append(send(red2.at[s], red2.at[s], r2s_sem.at[d - 1], r2r_sem.at[d - 1], (b, sector(d))))
        reduce2[-1].start()

    bwd = []
    for n in range(feat // nbk):
        rows = slice(n * nbk, (n + 1) * nbk)
        part = nt(hidden[...], win[rows, :]).reshape(lat_n, lon_n, nbk)
        gmix[:, :, rows] = part
        for side, rim in enumerate(
            (gmix[last_i, :, rows], gmix[0, :, rows], gmix[:, last_j, rows], gmix[:, 0, rows])
        ):
            bedge_s[n, side] = rim.astype(BF16)
        for side, (ci, cj) in enumerate(((last_i, last_j), (last_i, 0), (0, last_j), (0, 0))):
            bcorn_s[n, side] = gmix[ci, cj : cj + 1, rows]
        sent = []
        for side in range(4):
            sent.append(
                send(
                    bedge_s.at[n, side], bedge_r.at[n, side],
                    bs_sem.at[n, side], br_sem.at[n, side], edge_to[side],
                )
            )
        for side in range(4):
            sent.append(
                send(
                    bcorn_s.at[n, side], bcorn_r.at[n, side],
                    bs_sem.at[n, 4 + side], br_sem.at[n, 4 + side], corner_to[side],
                )
            )
        for copy in sent:
            copy.start()
        bwd.append(sent)

    for copy in reduce2:
        copy.wait_recv()
    total = red2[0]
    for d in range(1, ns):
        total = total + red2[d]
    total = jnp.sum(total, axis=1, keepdims=True)
    alpha = total[0:1] / total[1:2]

    for n in range(feat // nbk):
        for copy in bwd[n]:
            copy.wait_recv()

        def unmix(k, carry):
            cols = pl.ds(pl.multiple_of(n * nbk + k * cw, cw), cw)
            inner = pl.ds(pl.multiple_of(k * cw, cw), cw)
            taps = [coef[8 - t : 9 - t, cols] for t in range(9)]

            def row(r):
                if r < 0:
                    return bedge_r[n, 0, :, inner].astype(F32) * north
                if r == lat_n:
                    return bedge_r[n, 1, :, inner].astype(F32) * south
                return gmix[r, :, cols]

            corners = [bcorn_r[n, side, :, inner] * (north if side < 2 else south) for side in range(4)]
            west = bedge_r[n, 2, :, inner].astype(F32)
            east = bedge_r[n, 3, :, inner].astype(F32)
            for i, summed in enumerate(stencil_rows(row, west, east, corners, taps, lat_n, lon_n)):
                hess = direc[i, :, cols] + obs[i * lon_n : (i + 1) * lon_n, cols] + summed
                out_ref[i, :, cols] = res[i, :, cols] - alpha * hess
            return carry

        lax.fori_loop(0, nbk // cw, unmix, 0)

    for copy in fwd + phase1 + phase2 + reduce1 + reduce2 + [copy for sent in bwd for copy in sent]:
        copy.wait_send()


def shards(
    nb, ns,
    base_state, direction, residual, mix_coef, w_in, w_out,
    obs_patch, obs_count, obs_pos, obs_wgt, obs_rinv,
):
    lat_n, lon_n, feat = base_state.shape
    hid = w_in.shape[1]
    slot_n, tap_n = obs_pos.shape[2:]
    tok_n = lat_n * lon_n
    block_n = nb * ns
    n1 = min(512, hid)
    n2 = min(512, feat)
    nbk = min(512, feat)
    patch = obs_patch[0].T
    count = obs_count
    pos = jnp.transpose(obs_pos[0], (1, 2, 0)).reshape(slot_n * tap_n, block_n)
    wgt = jnp.transpose(obs_wgt[0], (1, 2, 0)).reshape(slot_n * tap_n, block_n)
    rinv = obs_rinv[0].T
    stations = slot_n * block_n
    dma = pltpu.SemaphoreType.DMA
    vmem = pltpu.VMEM
    chunks = feat // nbk
    scratch = [
        vmem((lat_n, lon_n, feat), F32), vmem((lat_n, lon_n, feat), F32), vmem((lat_n, lon_n, feat), F32),
        vmem(mix_coef.shape, F32), vmem(w_in.shape, BF16), vmem(w_out.shape, BF16),
        vmem(patch.shape, jnp.int32), vmem(count.shape, jnp.int32), vmem(pos.shape, jnp.int32),
        vmem(wgt.shape, F32), vmem(rinv.shape, F32),
        vmem((2 * tok_n, feat), BF16), vmem((tok_n, hid), F32), vmem((tok_n, hid), BF16),
        vmem((tok_n, feat), BF16), vmem((stations, feat), F32), vmem((stations, tok_n), BF16),
        vmem((8, LANES), F32), vmem((tok_n, feat), F32), vmem((tok_n, feat), BF16),
        vmem((lat_n, lon_n, feat), F32),
        vmem((4, 2, 16, feat), BF16), vmem((4, 2, 16, feat), BF16),
        vmem((4, 2, feat), F32), vmem((4, 2, feat), F32),
        vmem((chunks, 4, 16, nbk), BF16), vmem((chunks, 4, 16, nbk), BF16),
        vmem((chunks, 4, 1, nbk), F32), vmem((chunks, 4, 1, nbk), F32),
        vmem((LANES, block_n), F32), vmem((nb, ns, LANES), F32), vmem((nb, ns, LANES), F32),
        vmem((ns, nb, LANES), F32), vmem((ns, nb, LANES), F32),
        vmem((2, LANES), F32), vmem((nb, 2, LANES), F32), vmem((ns, 2, LANES), F32),
        dma((9,)), dma((hid // n1,)), dma((feat // n2,)),
        dma((8,)), dma((8,)), dma((chunks, 8)), dma((chunks, 8)),
        dma((nb - 1,)), dma((nb - 1,)), dma((ns - 1,)), dma((ns - 1,)),
        dma((nb - 1,)), dma((nb - 1,)), dma((ns - 1,)), dma((ns - 1,)),
    ]
    sizes = (nb, ns, lat_n, lon_n, feat, hid, slot_n, tap_n, n1, n2, nbk)
    return pl.pallas_call(
        functools.partial(kernel, sizes),
        out_shape=jax.ShapeDtypeStruct(base_state.shape, F32),
        in_specs=[pl.BlockSpec(memory_space=pl.ANY)] * 11,
        out_specs=pl.BlockSpec(memory_space=pltpu.VMEM),
        scratch_shapes=scratch,
        compiler_params=pltpu.CompilerParams(
            collective_id=0, has_side_effects=True, vmem_limit_bytes=60 * 2**20
        ),
    )(base_state, direction, residual, mix_coef, w_in, w_out, patch, count, pos, wgt, rinv)


def solution(mesh):
    return jax.shard_map(
        functools.partial(shards, mesh.shape["band"], mesh.shape["sector"]),
        mesh=mesh,
        in_specs=(
            P("band", "sector", None),
            P("band", "sector", None),
            P("band", "sector", None),
            P(),
            P(),
            P(),
            P(("band", "sector"), None, None),
            P(("band", "sector"), None),
            P(("band", "sector"), None, None, None),
            P(("band", "sector"), None, None, None),
            P(("band", "sector"), None, None),
        ),
        out_specs=P("band", "sector", None),
        check_vma=False,
    )
```

```python
import functools
import math

import jax
import jax.numpy as jnp
from jax import lax
from jax.experimental import pallas as pl
from jax.experimental.pallas import tpu as pltpu
from jax.sharding import PartitionSpec as P

MESH = pl.DeviceIdType.MESH
F32 = jnp.float32
BF16 = jnp.bfloat16
LANES = 128


def gelu_slope(preact):
    normal_cdf = 0.5 * (1.0 + lax.erf(preact * (1.0 / math.sqrt(2.0))))
    normal_pdf = jnp.exp(-0.5 * preact * preact) * (1.0 / math.sqrt(2.0 * math.pi))
    return normal_cdf + preact * normal_pdf


def nn(left, right):
    return jnp.dot(left, right, preferred_element_type=F32)


def nt(left, right):
    return lax.dot_general(left, right, (((1,), (1,)), ((), ())), preferred_element_type=F32)


def tn(left, right):
    return lax.dot_general(left, right, (((0,), (0,)), ((), ())), preferred_element_type=F32)


def fold_lanes(values):
    total = values[:, :LANES]
    for at in range(LANES, values.shape[1], LANES):
        total = total + values[:, at : at + LANES]
    return total


def shifted(part, lon_n):
    lon_at = lax.broadcasted_iota(jnp.int32, part[0].shape, 0)
    low = jnp.where(lon_at == 0, 0.0, pltpu.roll(part[0], 1, 0))
    high = jnp.where(lon_at == lon_n - 1, 0.0, pltpu.roll(part[2], lon_n - 1, 0))
    return low + part[1] + high


def inner_rows(row, coef, lat_n, lon_n):
    before, now = None, row(0)
    for i in range(lat_n):
        after = row(i + 1) if i < lat_n - 1 else None
        part = []
        for b in range(3):
            summed = coef[3 + b] * now
            if before is not None:
                summed = summed + coef[b] * before
            if after is not None:
                summed = summed + coef[6 + b] * after
            part.append(summed)
        yield shifted(part, lon_n)
        before, now = now, after


def rim_rows(north, south, west, east, corners, coef, lat_n, lon_n):
    width = west.shape[1]
    lat_at = lax.broadcasted_iota(jnp.int32, (lat_n, width), 0)
    lon_at = lax.broadcasted_iota(jnp.int32, (lon_n, width), 0)

    def column(mid, above, below, b):
        prev = jnp.where(lat_at == 0, above, pltpu.roll(mid, 1, 0))
        following = jnp.where(lat_at == lat_n - 1, below, pltpu.roll(mid, lat_n - 1, 0))
        return coef[b] * prev + coef[3 + b] * mid + coef[6 + b] * following

    rim_w = column(west, corners[0], corners[2], 0)
    rim_e = column(east, corners[1], corners[3], 2)
    for i in range(lat_n):
        rim = jnp.where(lon_at == 0, rim_w[i : i + 1], 0.0) + jnp.where(lon_at == lon_n - 1, rim_e[i : i + 1], 0.0)
        if i == 0:
            rim = rim + shifted([coef[b] * north for b in range(3)], lon_n)
        if i == lat_n - 1:
            rim = rim + shifted([coef[6 + b] * south for b in range(3)], lon_n)
        yield rim


def kernel(
    sizes,
    base_h, dir_h, res_h, coef_h, win_h, wout_h, patch_h, count_h, pos_h, wgt_h, rinv_h,
    out_ref,
    base, direc, res, coef, win, wout, patch, count, pos, wgt, rinv,
    acc, mixed, slopes, hidden, tang, weights, onehot, obs, obs_b, gmix,
    fedge_s, fedge_r, fcorn_s, fcorn_r, bedge_s, bedge_r, bcorn_s, bcorn_r,
    pay, a0, a1, a2, a3, red0, red1, red2,
    load_sem, fs_sem, fr_sem, bs_sem, br_sem,
    p1s_sem, p1r_sem, p2s_sem, p2r_sem, r1s_sem, r1r_sem, r2s_sem, r2r_sem,
):
    nb, ns, lat_n, lon_n, feat, hid, slot_n, tap_n, n1, n2, nbk, cw = sizes
    tok_n = lat_n * lon_n
    block_n = nb * ns
    last_i, last_j = lat_n - 1, lon_n - 1
    b = lax.axis_index("band")
    s = lax.axis_index("sector")

    def band(step):
        return lax.rem(b + step + nb, nb)

    def sector(step):
        return lax.rem(s + step + ns, ns)

    edge_to = [(band(1), s), (band(-1), s), (b, sector(1)), (b, sector(-1))]
    corner_to = [
        (band(1), sector(1)), (band(1), sector(-1)), (band(-1), sector(1)), (band(-1), sector(-1)),
    ]
    partners = [(band(d), s) for d in range(1, nb)] + [(b, sector(d)) for d in range(1, ns)] + corner_to
    barrier = pltpu.get_barrier_semaphore()
    for partner in partners:
        pl.semaphore_signal(barrier, inc=1, device_id=partner, device_id_type=MESH)

    loads = {}
    pairs = dict(
        base=(base_h, base), dir=(dir_h, direc),
        patch=(patch_h, patch), count=(count_h, count), pos=(pos_h, pos), wgt=(wgt_h, wgt), rinv=(rinv_h, rinv),
        coef=(coef_h, coef), win=(win_h, win), res=(res_h, res), wout=(wout_h, wout),
    )
    for at, (name, (src, dst)) in enumerate(pairs.items()):
        loads[name] = pltpu.make_async_copy(src, dst, load_sem.at[at])
        loads[name].start()

    def send(src, dst, send_sem, recv_sem, to):
        copy = pltpu.make_async_remote_copy(
            src_ref=src, dst_ref=dst, send_sem=send_sem, recv_sem=recv_sem, device_id=to, device_id_type=MESH
        )
        copy.start()
        return copy

    rim_at = ((last_i, last_j), (last_i, 0), (0, last_j), (0, 0))
    for at, (name, field) in enumerate((("base", base), ("dir", direc))):
        loads[name].wait()
        for side, rim in enumerate((field[last_i], field[0], field[:, last_j], field[:, 0])):
            fedge_s[at, side] = rim.astype(BF16)
        for side, (ci, cj) in enumerate(rim_at):
            fcorn_s[at, side] = field[ci, cj : cj + 1]
    pl.semaphore_wait(barrier, len(partners))
    fwd = []
    for at in range(2):
        sent = []
        for side in range(4):
            sent.append(
                send(
                    fedge_s.at[at, side], fedge_r.at[at, side],
                    fs_sem.at[at, side], fr_sem.at[at, side], edge_to[side],
                )
            )
        for side in range(4):
            sent.append(
                send(
                    fcorn_s.at[at, side], fcorn_r.at[at, side],
                    fs_sem.at[at, 4 + side], fr_sem.at[at, 4 + side], corner_to[side],
                )
            )
        fwd.append(sent)

    for name in ("patch", "count", "pos", "wgt", "rinv"):
        loads[name].wait()
    slot_at = lax.broadcasted_iota(jnp.int32, (slot_n, block_n), 0)
    tap_all = slot_n * tap_n
    pay[...] = jnp.zeros_like(pay)
    pay[0:slot_n] = patch[...].astype(F32)
    pay[slot_n : 2 * slot_n] = jnp.where(slot_at < count[...], rinv[...], 0.0)
    pay[2 * slot_n : 2 * slot_n + tap_all] = pos[...].astype(F32)
    pay[2 * slot_n + tap_all : 2 * slot_n + 2 * tap_all] = wgt[...]
    a0[...] = jnp.transpose(pay[...]).reshape(nb, ns, LANES)
    a1[b] = a0[b]
    phase1 = []
    for d in range(1, nb):
        phase1.append(send(a0.at[band(d)], a1.at[b], p1s_sem.at[d - 1], p1r_sem.at[d - 1], (band(d), s)))

    loads["coef"].wait()
    for at, field in enumerate((base, direc)):
        def premix(k, carry, at=at, field=field):
            cols = pl.ds(pl.multiple_of(k * cw, cw), cw)
            taps = [coef[t : t + 1, cols] for t in range(9)]
            for i, summed in enumerate(inner_rows(lambda r: field[r, :, cols], taps, lat_n, lon_n)):
                acc[at, i, :, cols] = summed
            return carry

        lax.fori_loop(0, feat // cw, premix, 0)

    loads["res"].wait()
    zero = jnp.zeros((lon_n, LANES), F32)

    def square(i, carry):
        norm, grow = carry
        r, d = res[i], direc[i]
        return norm + fold_lanes(r * r), grow + fold_lanes(d * d)

    norm, grow = lax.fori_loop(0, lat_n, square, (zero, zero))
    red0[0:1] = jnp.sum(norm, axis=0, keepdims=True)
    red0[1:2] = jnp.sum(grow, axis=0, keepdims=True)

    inside_n = (b > 0).astype(F32)
    inside_s = (b < nb - 1).astype(F32)

    def rims_in(edge, corn, taps, cols):
        corners = [corn.at[side][:, cols] * (inside_n if side < 2 else inside_s) for side in range(4)]
        north = edge.at[0][:, cols].astype(F32) * inside_n
        south = edge.at[1][:, cols].astype(F32) * inside_s
        west = edge.at[2][:, cols].astype(F32)
        east = edge.at[3][:, cols].astype(F32)
        return rim_rows(north, south, west, east, corners, taps, lat_n, lon_n)

    def postmix(at, cols):
        taps = [coef[t : t + 1, cols] for t in range(9)]
        for i, rim in enumerate(rims_in(fedge_r.at[at], fcorn_r.at[at], taps, cols)):
            start = at * tok_n + i * lon_n
            mixed[start : start + lon_n, cols] = (acc[at, i, :, cols] + rim).astype(BF16)

    for copy in fwd[0]:
        copy.wait_recv()

    def postmix_base(k, carry):
        postmix(0, pl.ds(pl.multiple_of(k * cw, cw), cw))
        return carry

    lax.fori_loop(0, feat // cw, postmix_base, 0)
    loads["win"].wait()

    phase2 = []
    posts = [slice(k * cw, (k + 1) * cw) for k in range(feat // cw)]
    half = hid // n1 // 2
    for n in range(hid // n1):
        cols = slice(n * n1, (n + 1) * n1)
        slopes[:, cols] = gelu_slope(nn(mixed[:tok_n], win[:, cols]))
        if n == 0:
            for copy in phase1:
                copy.wait_recv()
            for q in range(ns):
                a2[q] = a1[:, q, :]
            a3[s] = a2[s]
            for d in range(1, ns):
                phase2.append(
                    send(a2.at[sector(d)], a3.at[s], p2s_sem.at[d - 1], p2r_sem.at[d - 1], (b, sector(d)))
                )
        if n == half - 1:
            for copy in fwd[1]:
                copy.wait_recv()
        if n >= half:
            share = -(-len(posts) // (hid // n1 - half))
            for part in posts[(n - half) * share : (n - half + 1) * share]:
                postmix(1, part)

    stations = slot_n * block_n
    rb = min(32, block_n)
    blocks = [(c, r) for c in range(slot_n) for r in range(0, block_n, rb)]

    def place(c):
        told = a3[...].reshape(block_n, LANES)
        cell_at = lax.broadcasted_iota(jnp.int32, (block_n, tok_n), 1).astype(F32)
        onehot[c * block_n : (c + 1) * block_n] = jnp.where(told[:, c : c + 1] == cell_at, 1.0, 0.0).astype(BF16)

    def spread(c, r):
        rows = a3[r // nb : (r + rb) // nb].reshape(rb, LANES)
        lane_at = lax.broadcasted_iota(jnp.int32, (rb, LANES), 1).astype(F32)
        first = 2 * slot_n + c * tap_n
        chans = [jnp.broadcast_to(rows[:, first + k : first + k + 1], (rb, LANES)) for k in range(tap_n)]
        first += tap_all
        wgts = [jnp.broadcast_to(rows[:, first + k : first + k + 1], (rb, LANES)) for k in range(tap_n)]
        for j in range(feat // LANES):
            here = lane_at + float(j * LANES)
            summed = jnp.where(chans[0] == here, wgts[0], 0.0)
            for k in range(1, tap_n):
                summed = summed + jnp.where(chans[k] == here, wgts[k], 0.0)
            weights[c * block_n + r : c * block_n + r + rb, j * LANES : (j + 1) * LANES] = summed

    steps = hid // n1
    for n in range(steps):
        cols = slice(n * n1, (n + 1) * n1)
        hidden[:, cols] = (slopes[:, cols] * nn(mixed[tok_n:], win[:, cols])).astype(BF16)
        if n == half:
            for copy in phase2:
                copy.wait_recv()
            loads["wout"].wait()
        if n > half:
            share = -(-len(blocks) // (steps - half - 1))
            for c, r in blocks[(n - half - 1) * share : (n - half) * share]:
                spread(c, r)
    for c in range(slot_n):
        place(c)

    seen = jnp.zeros((stations, LANES), F32)
    for n in range(feat // n2):
        cols = slice(n * n2, (n + 1) * n2)
        own = direc[:, :, cols].reshape(tok_n, n2)
        tang[:, cols] = (own + nn(hidden[...], wout[:, cols])).astype(BF16)
        sampled = nn(onehot[...], tang[:, cols])
        seen = seen + fold_lanes(sampled * weights[:, cols])
    misfit = jnp.sum(seen, axis=1, keepdims=True)
    told = a3[...].reshape(block_n, LANES)
    inverse = jnp.concatenate([told[:, slot_n + c : slot_n + c + 1] for c in range(slot_n)], axis=0)
    scaled = inverse * misfit
    lane0 = lax.broadcasted_iota(jnp.int32, (1, LANES), 1) == 0
    red0[1:2] = red0[1:2] + jnp.where(lane0, jnp.sum(scaled * misfit, axis=0, keepdims=True), 0.0)

    reduce1 = []
    red1[b] = red0[...]
    for d in range(1, nb):
        reduce1.append(send(red0, red1.at[b], r1s_sem.at[d - 1], r1r_sem.at[d - 1], (band(d), s)))

    for n in range(feat // n2):
        cols = slice(n * n2, (n + 1) * n2)
        deposit = scaled * weights[:, cols]
        rough = deposit.astype(BF16)
        fine = (deposit - rough.astype(F32)).astype(BF16)
        summed = tn(onehot[...], rough) + tn(onehot[...], fine)
        obs[:, cols] = summed
        obs_b[:, cols] = summed.astype(BF16)

    reduce2 = []
    for n in range(hid // n1):
        rows = slice(n * n1, (n + 1) * n1)
        hidden[:, rows] = (slopes[:, rows] * nt(obs_b[...], wout[rows, :])).astype(BF16)
        if n == half - 1:
            for copy in reduce1:
                copy.wait_recv()
            total = red1[0]
            for d in range(1, nb):
                total = total + red1[d]
            red2[s] = total
            for d in range(1, ns):
                reduce2.append(
                    send(red2.at[s], red2.at[s], r2s_sem.at[d - 1], r2r_sem.at[d - 1], (b, sector(d)))
                )

    bwd = []
    for n in range(feat // nbk):
        rows = slice(n * nbk, (n + 1) * nbk)
        part = nt(hidden[...], win[rows, :]).reshape(lat_n, lon_n, nbk)
        gmix[:, :, rows] = part
        for side, rim in enumerate(
            (gmix[last_i, :, rows], gmix[0, :, rows], gmix[:, last_j, rows], gmix[:, 0, rows])
        ):
            bedge_s[n, side] = rim.astype(BF16)
        for side, (ci, cj) in enumerate(rim_at):
            bcorn_s[n, side] = gmix[ci, cj : cj + 1, rows]
        sent = []
        for side in range(4):
            sent.append(
                send(
                    bedge_s.at[n, side], bedge_r.at[n, side],
                    bs_sem.at[n, side], br_sem.at[n, side], edge_to[side],
                )
            )
        for side in range(4):
            sent.append(
                send(
                    bcorn_s.at[n, side], bcorn_r.at[n, side],
                    bs_sem.at[n, 4 + side], br_sem.at[n, 4 + side], corner_to[side],
                )
            )
        bwd.append(sent)

    def preunmix(k, carry):
        cols = pl.ds(pl.multiple_of(k * cw, cw), cw)
        taps = [coef[8 - t : 9 - t, cols] for t in range(9)]
        for i, summed in enumerate(inner_rows(lambda r: gmix[r, :, cols], taps, lat_n, lon_n)):
            acc[0, i, :, cols] = direc[i, :, cols] + obs[i * lon_n : (i + 1) * lon_n, cols] + summed
        return carry

    lax.fori_loop(0, feat // cw, preunmix, 0)

    for copy in reduce2:
        copy.wait_recv()
    total = red2[0]
    for d in range(1, ns):
        total = total + red2[d]
    total = jnp.sum(total, axis=1, keepdims=True)
    alpha = total[0:1] / total[1:2]

    for n in range(feat // nbk):
        for copy in bwd[n]:
            copy.wait_recv()

        def unmix(k, carry):
            cols = pl.ds(pl.multiple_of(n * nbk + k * cw, cw), cw)
            inner = pl.ds(pl.multiple_of(k * cw, cw), cw)
            taps = [coef[8 - t : 9 - t, cols] for t in range(9)]
            for i, rim in enumerate(rims_in(bedge_r.at[n], bcorn_r.at[n], taps, inner)):
                out_ref[i, :, cols] = res[i, :, cols] - alpha * (acc[0, i, :, cols] + rim)
            return carry

        lax.fori_loop(0, nbk // cw, unmix, 0)

    for sent in fwd + [phase1, phase2, reduce1, reduce2] + bwd:
        for copy in sent:
            copy.wait_send()


def shards(
    nb, ns,
    base_state, direction, residual, mix_coef, w_in, w_out,
    obs_patch, obs_count, obs_pos, obs_wgt, obs_rinv,
):
    lat_n, lon_n, feat = base_state.shape
    hid = w_in.shape[1]
    slot_n, tap_n = obs_pos.shape[2:]
    tok_n = lat_n * lon_n
    block_n = nb * ns
    n1 = min(512, hid)
    n2 = min(512, feat)
    nbk = min(512, feat)
    patch = obs_patch[0].T
    count = obs_count
    pos = jnp.transpose(obs_pos[0], (1, 2, 0)).reshape(slot_n * tap_n, block_n)
    wgt = jnp.transpose(obs_wgt[0], (1, 2, 0)).reshape(slot_n * tap_n, block_n)
    rinv = obs_rinv[0].T
    stations = slot_n * block_n
    dma = pltpu.SemaphoreType.DMA
    vmem = pltpu.VMEM
    chunks = feat // nbk
    cw = min(256, nbk)
    scratch = [
        vmem((lat_n, lon_n, feat), F32), vmem((lat_n, lon_n, feat), F32), vmem((lat_n, lon_n, feat), F32),
        vmem(mix_coef.shape, F32), vmem(w_in.shape, BF16), vmem(w_out.shape, BF16),
        vmem(patch.shape, jnp.int32), vmem(count.shape, jnp.int32), vmem(pos.shape, jnp.int32),
        vmem(wgt.shape, F32), vmem(rinv.shape, F32),
        vmem((2, lat_n, lon_n, feat), F32), vmem((2 * tok_n, feat), BF16), vmem((tok_n, hid), F32),
        vmem((tok_n, hid), BF16), vmem((tok_n, feat), BF16), vmem((stations, feat), F32),
        vmem((stations, tok_n), BF16), vmem((tok_n, feat), F32), vmem((tok_n, feat), BF16),
        vmem((lat_n, lon_n, feat), F32),
        vmem((2, 4, 16, feat), BF16), vmem((2, 4, 16, feat), BF16),
        vmem((2, 4, 1, feat), F32), vmem((2, 4, 1, feat), F32),
        vmem((chunks, 4, 16, nbk), BF16), vmem((chunks, 4, 16, nbk), BF16),
        vmem((chunks, 4, 1, nbk), F32), vmem((chunks, 4, 1, nbk), F32),
        vmem((LANES, block_n), F32), vmem((nb, ns, LANES), F32), vmem((nb, ns, LANES), F32),
        vmem((ns, nb, LANES), F32), vmem((ns, nb, LANES), F32),
        vmem((2, LANES), F32), vmem((nb, 2, LANES), F32), vmem((ns, 2, LANES), F32),
        dma((11,)), dma((2, 8)), dma((2, 8)), dma((chunks, 8)), dma((chunks, 8)),
        dma((nb - 1,)), dma((nb - 1,)), dma((ns - 1,)), dma((ns - 1,)),
        dma((nb - 1,)), dma((nb - 1,)), dma((ns - 1,)), dma((ns - 1,)),
    ]
    sizes = (nb, ns, lat_n, lon_n, feat, hid, slot_n, tap_n, n1, n2, nbk, cw)
    return pl.pallas_call(
        functools.partial(kernel, sizes),
        out_shape=pltpu.VMEM(base_state.shape, F32),
        in_specs=[pl.BlockSpec(memory_space=pl.ANY)] * 11,
        out_specs=pl.BlockSpec(memory_space=pltpu.VMEM),
        scratch_shapes=scratch,
        compiler_params=pltpu.CompilerParams(
            collective_id=0, has_side_effects=True, vmem_limit_bytes=56 * 2**20
        ),
    )(base_state, direction, residual, mix_coef, w_in, w_out, patch, count, pos, wgt, rinv)


def solution(mesh):
    return jax.shard_map(
        functools.partial(shards, mesh.shape["band"], mesh.shape["sector"]),
        mesh=mesh,
        in_specs=(
            P("band", "sector", None),
            P("band", "sector", None),
            P("band", "sector", None),
            P(),
            P(),
            P(),
            P(("band", "sector"), None, None),
            P(("band", "sector"), None),
            P(("band", "sector"), None, None, None),
            P(("band", "sector"), None, None, None),
            P(("band", "sector"), None, None),
        ),
        out_specs=P("band", "sector", None),
        check_vma=False,
    )
```

```python
import functools
import math

import jax
import jax.numpy as jnp
from jax import lax
from jax.experimental import pallas as pl
from jax.experimental.pallas import tpu as pltpu
from jax.sharding import PartitionSpec as P

MESH = pl.DeviceIdType.MESH
F32 = jnp.float32
BF16 = jnp.bfloat16
LANES = 128


def gelu_slope(preact):
    normal_cdf = 0.5 * (1.0 + lax.erf(preact * (1.0 / math.sqrt(2.0))))
    normal_pdf = jnp.exp(-0.5 * preact * preact) * (1.0 / math.sqrt(2.0 * math.pi))
    return normal_cdf + preact * normal_pdf


def nn(left, right):
    return jnp.dot(left, right, preferred_element_type=F32)


def nt(left, right):
    return lax.dot_general(left, right, (((1,), (1,)), ((), ())), preferred_element_type=F32)


def tn(left, right):
    return lax.dot_general(left, right, (((0,), (0,)), ((), ())), preferred_element_type=F32)


def fold_lanes(values):
    total = values[:, :LANES]
    for at in range(LANES, values.shape[1], LANES):
        total = total + values[:, at : at + LANES]
    return total


def shifted(part, lon_n):
    lon_at = lax.broadcasted_iota(jnp.int32, part[0].shape, 0)
    low = jnp.where(lon_at == 0, 0.0, pltpu.roll(part[0], 1, 0))
    high = jnp.where(lon_at == lon_n - 1, 0.0, pltpu.roll(part[2], lon_n - 1, 0))
    return low + part[1] + high


def inner_rows(row, coef, lat_n, lon_n):
    before, now = None, row(0)
    for i in range(lat_n):
        after = row(i + 1) if i < lat_n - 1 else None
        part = []
        for b in range(3):
            summed = coef[3 + b] * now
            if before is not None:
                summed = summed + coef[b] * before
            if after is not None:
                summed = summed + coef[6 + b] * after
            part.append(summed)
        yield shifted(part, lon_n)
        before, now = now, after


def rim_shares(north, south, west, east, corners, coef, lat_n, lon_n):
    lat_at = lax.broadcasted_iota(jnp.int32, (lat_n, west.shape[1]), 0)

    def column(mid, above, below, b):
        prev = jnp.where(lat_at == 0, above, pltpu.roll(mid, 1, 0))
        following = jnp.where(lat_at == lat_n - 1, below, pltpu.roll(mid, lat_n - 1, 0))
        return coef[b] * prev + coef[3 + b] * mid + coef[6 + b] * following

    rim_w = column(west, corners[0], corners[2], 0)
    rim_e = column(east, corners[1], corners[3], 2)
    first = shifted([coef[b] * north for b in range(3)], lon_n)
    last = shifted([coef[6 + b] * south for b in range(3)], lon_n)
    return first, last, rim_w, rim_e


def kernel(
    sizes,
    base_h, dir_h, res_h, coef_h, win_h, wout_h, patch_h, count_h, pos_h, wgt_h, rinv_h,
    out_ref,
    base, direc, res, coef, win, wout, patch, count, pos, wgt, rinv,
    acc, mixed, rimmed, slopes, hidden, tang, weights, onehot, obs, obs_b, gmix,
    fedge_s, fedge_r, fcorn_s, fcorn_r, bedge_s, bedge_r, bcorn_s, bcorn_r,
    pay, a0, a1, a2, a3, red0, red1, red2,
    load_sem, fs_sem, fr_sem, bs_sem, br_sem, ps_sem, pr_sem,
):
    nb, ns, lat_n, lon_n, feat, hid, slot_n, tap_n, n1, n2, nbk, cw, nw = sizes
    tok_n = lat_n * lon_n
    rim_n = 2 * (lat_n + lon_n)
    block_n = nb * ns
    last_i, last_j = lat_n - 1, lon_n - 1
    b = lax.axis_index("band")
    s = lax.axis_index("sector")

    def band(step):
        return lax.rem(b + step + nb, nb)

    def sector(step):
        return lax.rem(s + step + ns, ns)

    edge_to = [(band(1), s), (band(-1), s), (b, sector(1)), (b, sector(-1))]
    corner_to = [
        (band(1), sector(1)), (band(1), sector(-1)), (band(-1), sector(1)), (band(-1), sector(-1)),
    ]
    partners = [(band(d), s) for d in range(1, nb)] + [(b, sector(d)) for d in range(1, ns)] + corner_to
    barrier = pltpu.get_barrier_semaphore()
    for partner in partners:
        pl.semaphore_signal(barrier, inc=1, device_id=partner, device_id_type=MESH)

    loads = {}
    pairs = dict(
        base=(base_h, base), dir=(dir_h, direc), coef=(coef_h, coef),
        patch=(patch_h, patch), count=(count_h, count), pos=(pos_h, pos), wgt=(wgt_h, wgt), rinv=(rinv_h, rinv),
    )
    for n in range(hid // nw):
        cols = pl.ds(n * nw, nw)
        pairs[n] = (win_h.at[:, cols], win.at[:, cols])
    pairs |= dict(res=(res_h, res), wout=(wout_h, wout))
    for at, (name, (src, dst)) in enumerate(pairs.items()):
        loads[name] = pltpu.make_async_copy(src, dst, load_sem.at[at])
        loads[name].start()

    def send(src, dst, send_sem, recv_sem, to):
        copy = pltpu.make_async_remote_copy(
            src_ref=src, dst_ref=dst, send_sem=send_sem, recv_sem=recv_sem, device_id=to, device_id_type=MESH
        )
        copy.start()

    def landed(buffer, sem):
        pltpu.make_async_copy(buffer, buffer, sem).wait()

    rim_at = ((last_i, last_j), (last_i, 0), (0, last_j), (0, 0))
    for at, (name, field) in enumerate((("base", base), ("dir", direc))):
        loads[name].wait()
        for side, rim in enumerate((field[last_i], field[0], field[:, last_j], field[:, 0])):
            fedge_s[at, side] = rim.astype(BF16)
        for side, (ci, cj) in enumerate(rim_at):
            fcorn_s[at, side] = field[ci, cj : cj + 1]
    pl.semaphore_wait(barrier, len(partners))
    for at in range(2):
        for side in range(4):
            send(fedge_s.at[at, side], fedge_r.at[at, side], fs_sem.at[0], fr_sem.at[0], edge_to[side])
            send(fcorn_s.at[at, side], fcorn_r.at[at, side], fs_sem.at[1], fr_sem.at[1], corner_to[side])

    for name in ("patch", "count", "pos", "wgt", "rinv"):
        loads[name].wait()
    slot_at = lax.broadcasted_iota(jnp.int32, (slot_n, block_n), 0)
    tap_all = slot_n * tap_n
    pay[...] = jnp.zeros_like(pay)
    pay[0:slot_n] = patch[...].astype(F32)
    pay[slot_n : 2 * slot_n] = jnp.where(slot_at < count[...], rinv[...], 0.0)
    pay[2 * slot_n : 2 * slot_n + tap_all] = pos[...].astype(F32)
    pay[2 * slot_n + tap_all : 2 * slot_n + 2 * tap_all] = wgt[...]
    a0[...] = jnp.transpose(pay[...]).reshape(nb, ns, LANES)

    a1[b] = a0[b]
    for d in range(1, nb):
        send(a0.at[band(d)], a1.at[b], ps_sem.at[0], pr_sem.at[0], (band(d), s))

    loads["coef"].wait()

    def premix(at, field, cols):
        taps = [coef[t : t + 1, cols] for t in range(9)]
        for i, summed in enumerate(inner_rows(lambda r: field[r, :, cols], taps, lat_n, lon_n)):
            acc[at, i, :, cols] = summed
            start = at * tok_n + i * lon_n
            mixed[start : start + lon_n, cols] = summed.astype(BF16)

    def premix_base(k, carry):
        premix(0, base, pl.ds(pl.multiple_of(k * cw, cw), cw))
        return carry

    lax.fori_loop(0, feat // cw, premix_base, 0)

    inside_n = (b > 0).astype(F32)
    inside_s = (b < nb - 1).astype(F32)

    def rims_in(edge, corn, taps, cols):
        corners = [corn.at[side][:, cols] * (inside_n if side < 2 else inside_s) for side in range(4)]
        north = edge.at[0][:, cols].astype(F32) * inside_n
        south = edge.at[1][:, cols].astype(F32) * inside_s
        west = edge.at[2][:, cols].astype(F32)
        east = edge.at[3][:, cols].astype(F32)
        return rim_shares(north, south, west, east, corners, taps, lat_n, lon_n)

    steps = hid // n1
    parts = feat // cw
    share = -(-parts // steps)
    for n in range(steps):
        if n * n1 % nw == 0:
            loads[n * n1 // nw].wait()
        cols = slice(n * n1, (n + 1) * n1)
        slopes[:, cols] = gelu_slope(nn(mixed[:tok_n], win[:, cols]))
        for k in range(n * share, min((n + 1) * share, parts)):
            premix(1, direc, slice(k * cw, (k + 1) * cw))
    for n in range(steps):
        cols = slice(n * n1, (n + 1) * n1)
        hidden[:, cols] = (slopes[:, cols] * nn(mixed[tok_n:], win[:, cols])).astype(BF16)
        if n == steps // 3:
            landed(a1.at[pl.ds(0, nb - 1)], pr_sem.at[0])
            for q in range(ns):
                a2[q] = a1[:, q, :]
            a3[s] = a2[s]
            for d in range(1, ns):
                send(a2.at[sector(d)], a3.at[s], ps_sem.at[1], pr_sem.at[1], (b, sector(d)))

    loads["res"].wait()
    zero = jnp.zeros((lon_n, LANES), F32)

    def square(i, carry):
        norm, grow = carry
        r, d = res[i], direc[i]
        return norm + fold_lanes(r * r), grow + fold_lanes(d * d)

    norm, grow = lax.fori_loop(0, lat_n, square, (zero, zero))
    red0[0:1] = jnp.sum(norm, axis=0, keepdims=True)
    red0[1:2] = jnp.sum(grow, axis=0, keepdims=True)

    landed(fedge_r, fr_sem.at[0])
    landed(fcorn_r, fr_sem.at[1])

    def postmix(k, carry):
        cols = pl.ds(pl.multiple_of(k * cw, cw), cw)
        taps = [coef[t : t + 1, cols] for t in range(9)]
        for at in range(2):
            first, last, rim_w, rim_e = rims_in(fedge_r.at[at], fcorn_r.at[at], taps, cols)
            lon_at = lax.broadcasted_iota(jnp.int32, first.shape, 0)
            rows = []
            for i, own in ((0, first), (last_i, last)):
                ends = jnp.where(lon_at == 0, rim_w[i : i + 1], 0.0) + jnp.where(lon_at == last_j, rim_e[i : i + 1], 0.0)
                rows.append(acc[at, i, :, cols] + own + ends)
            rows.append(acc[at, :, 0, cols] + rim_w)
            rows.append(acc[at, :, last_j, cols] + rim_e)
            start = at * rim_n
            for row in rows:
                rimmed[start : start + row.shape[0], cols] = row.astype(BF16)
                start += row.shape[0]
        return carry

    lax.fori_loop(0, feat // cw, postmix, 0)
    lon_at = lax.broadcasted_iota(jnp.int32, (lon_n, n1), 0)
    for n in range(steps):
        cols = slice(n * n1, (n + 1) * n1)
        both = nn(rimmed[...], win[:, cols])
        slope = gelu_slope(both[:rim_n])
        value = slope * both[rim_n:]
        slopes[:lon_n, cols] = slope[:lon_n]
        slopes[last_i * lon_n :, cols] = slope[lon_n : 2 * lon_n]
        hidden[:lon_n, cols] = value[:lon_n].astype(BF16)
        hidden[last_i * lon_n :, cols] = value[lon_n : 2 * lon_n].astype(BF16)
        at_w, at_e = 2 * lon_n, 2 * lon_n + lat_n
        for i in range(1, last_i):
            start = i * lon_n
            slopes[start : start + 1, cols] = slope[at_w + i : at_w + i + 1]
            slopes[start + last_j : start + lon_n, cols] = slope[at_e + i : at_e + i + 1]
            inner = hidden[start : start + lon_n, cols].astype(F32)
            inner = jnp.where(lon_at == 0, value[at_w + i : at_w + i + 1], inner)
            inner = jnp.where(lon_at == last_j, value[at_e + i : at_e + i + 1], inner)
            hidden[start : start + lon_n, cols] = inner.astype(BF16)

    stations = slot_n * block_n
    rb = min(32, block_n)
    blocks = [(c, r) for c in range(slot_n) for r in range(0, block_n, rb)]

    def place(c):
        told = a3[...].reshape(block_n, LANES)
        cell_at = lax.broadcasted_iota(jnp.int32, (block_n, tok_n), 1).astype(F32)
        onehot[c * block_n : (c + 1) * block_n] = jnp.where(told[:, c : c + 1] == cell_at, 1.0, 0.0).astype(BF16)

    def spread(c, r):
        rows = a3[r // nb : (r + rb) // nb].reshape(rb, LANES)
        lane_at = lax.broadcasted_iota(jnp.int32, (rb, LANES), 1).astype(F32)
        first = 2 * slot_n + c * tap_n
        chans = [jnp.broadcast_to(rows[:, first + k : first + k + 1], (rb, LANES)) for k in range(tap_n)]
        first += tap_all
        wgts = [jnp.broadcast_to(rows[:, first + k : first + k + 1], (rb, LANES)) for k in range(tap_n)]
        for j in range(feat // LANES):
            here = lane_at + float(j * LANES)
            summed = jnp.where(chans[0] == here, wgts[0], 0.0)
            for k in range(1, tap_n):
                summed = summed + jnp.where(chans[k] == here, wgts[k], 0.0)
            weights[c * block_n + r : c * block_n + r + rb, j * LANES : (j + 1) * LANES] = summed

    seen = jnp.zeros((stations, LANES), F32)
    loads["wout"].wait()
    for n in range(feat // n2):
        cols = slice(n * n2, (n + 1) * n2)
        own = direc[:, :, cols].reshape(tok_n, n2)
        tang[:, cols] = (own + nn(hidden[...], wout[:, cols])).astype(BF16)
        if n == max(feat // n2 - 2, 0):
            landed(a3.at[pl.ds(0, ns - 1)], pr_sem.at[1])
    for c, r in blocks:
        spread(c, r)
    for c in range(slot_n):
        place(c)
    for n in range(feat // n2):
        cols = slice(n * n2, (n + 1) * n2)
        sampled = nn(onehot[...], tang[:, cols])
        seen = seen + fold_lanes(sampled * weights[:, cols])
    misfit = jnp.sum(seen, axis=1, keepdims=True)
    told = a3[...].reshape(block_n, LANES)
    inverse = jnp.concatenate([told[:, slot_n + c : slot_n + c + 1] for c in range(slot_n)], axis=0)
    scaled = inverse * misfit
    lane0 = lax.broadcasted_iota(jnp.int32, (1, LANES), 1) == 0
    red0[1:2] = red0[1:2] + jnp.where(lane0, jnp.sum(scaled * misfit, axis=0, keepdims=True), 0.0)

    red1[b] = red0[...]
    for d in range(1, nb):
        send(red0, red1.at[b], ps_sem.at[2], pr_sem.at[2], (band(d), s))

    for n in range(feat // n2):
        cols = slice(n * n2, (n + 1) * n2)
        deposit = scaled * weights[:, cols]
        rough = deposit.astype(BF16)
        fine = (deposit - rough.astype(F32)).astype(BF16)
        summed = tn(onehot[...], rough) + tn(onehot[...], fine)
        obs[:, cols] = summed
        obs_b[:, cols] = summed.astype(BF16)

    for n in range(hid // n1):
        rows = slice(n * n1, (n + 1) * n1)
        hidden[:, rows] = (slopes[:, rows] * nt(obs_b[...], wout[rows, :])).astype(BF16)

    for n in range(feat // nbk):
        rows = slice(n * nbk, (n + 1) * nbk)
        part = nt(hidden[...], win[rows, :]).reshape(lat_n, lon_n, nbk)
        gmix[:, :, rows] = part
        for side, rim in enumerate(
            (gmix[last_i, :, rows], gmix[0, :, rows], gmix[:, last_j, rows], gmix[:, 0, rows])
        ):
            bedge_s[n, side] = rim.astype(BF16)
        for side, (ci, cj) in enumerate(rim_at):
            bcorn_s[n, side] = gmix[ci, cj : cj + 1, rows]
        for side in range(4):
            send(bedge_s.at[n, side], bedge_r.at[n, side], bs_sem.at[0], br_sem.at[0, n], edge_to[side])
            send(bcorn_s.at[n, side], bcorn_r.at[n, side], bs_sem.at[1], br_sem.at[1, n], corner_to[side])
        if n == 0:
            landed(red1.at[pl.ds(0, nb - 1)], pr_sem.at[2])
            total = red1[0]
            for d in range(1, nb):
                total = total + red1[d]
            red2[s] = total
            for d in range(1, ns):
                send(red2.at[s], red2.at[s], ps_sem.at[3], pr_sem.at[3], (b, sector(d)))

    def preunmix(k, carry):
        cols = pl.ds(pl.multiple_of(k * cw, cw), cw)
        taps = [coef[8 - t : 9 - t, cols] for t in range(9)]
        for i, summed in enumerate(inner_rows(lambda r: gmix[r, :, cols], taps, lat_n, lon_n)):
            acc[0, i, :, cols] = direc[i, :, cols] + obs[i * lon_n : (i + 1) * lon_n, cols] + summed
        return carry

    lax.fori_loop(0, feat // cw, preunmix, 0)

    landed(red2.at[pl.ds(0, ns - 1)], pr_sem.at[3])
    total = red2[0]
    for d in range(1, ns):
        total = total + red2[d]
    total = jnp.sum(total, axis=1, keepdims=True)
    alpha = total[0:1] / total[1:2]

    for n in range(feat // nbk):
        landed(bedge_r.at[n], br_sem.at[0, n])
        landed(bcorn_r.at[n], br_sem.at[1, n])

        def unmix(k, carry):
            cols = pl.ds(pl.multiple_of(n * nbk + k * cw, cw), cw)
            inner = pl.ds(pl.multiple_of(k * cw, cw), cw)
            taps = [coef[8 - t : 9 - t, cols] for t in range(9)]
            first, last, rim_w, rim_e = rims_in(bedge_r.at[n], bcorn_r.at[n], taps, inner)
            lon_at = lax.broadcasted_iota(jnp.int32, first.shape, 0)
            for i in range(lat_n):
                rim = jnp.where(lon_at == 0, rim_w[i : i + 1], 0.0) + jnp.where(lon_at == last_j, rim_e[i : i + 1], 0.0)
                if i == 0:
                    rim = rim + first
                if i == last_i:
                    rim = rim + last
                out_ref[i, :, cols] = res[i, :, cols] - alpha * (acc[0, i, :, cols] + rim)
            return carry

        lax.fori_loop(0, nbk // cw, unmix, 0)

    landed(fedge_s, fs_sem.at[0])
    landed(fcorn_s, fs_sem.at[1])
    landed(bedge_s, bs_sem.at[0])
    landed(bcorn_s, bs_sem.at[1])
    landed(a1.at[pl.ds(0, nb - 1)], ps_sem.at[0])
    landed(a3.at[pl.ds(0, ns - 1)], ps_sem.at[1])
    landed(red1.at[pl.ds(0, nb - 1)], ps_sem.at[2])
    landed(red2.at[pl.ds(0, ns - 1)], ps_sem.at[3])


def shards(
    nb, ns,
    base_state, direction, residual, mix_coef, w_in, w_out,
    obs_patch, obs_count, obs_pos, obs_wgt, obs_rinv,
):
    lat_n, lon_n, feat = base_state.shape
    hid = w_in.shape[1]
    slot_n, tap_n = obs_pos.shape[2:]
    tok_n = lat_n * lon_n
    block_n = nb * ns
    n1 = min(512, hid)
    n2 = min(512, feat)
    nbk = min(512, feat)
    patch = obs_patch[0].T
    count = obs_count
    pos = jnp.transpose(obs_pos[0], (1, 2, 0)).reshape(slot_n * tap_n, block_n)
    wgt = jnp.transpose(obs_wgt[0], (1, 2, 0)).reshape(slot_n * tap_n, block_n)
    rinv = obs_rinv[0].T
    stations = slot_n * block_n
    dma = pltpu.SemaphoreType.DMA
    vmem = pltpu.VMEM
    chunks = feat // nbk
    cw = min(256, nbk)
    nw = 2 * n1 if hid % (2 * n1) == 0 else n1
    scratch = [
        vmem((lat_n, lon_n, feat), F32), vmem((lat_n, lon_n, feat), F32), vmem((lat_n, lon_n, feat), F32),
        vmem(mix_coef.shape, F32), vmem(w_in.shape, BF16), vmem(w_out.shape, BF16),
        vmem(patch.shape, jnp.int32), vmem(count.shape, jnp.int32), vmem(pos.shape, jnp.int32),
        vmem(wgt.shape, F32), vmem(rinv.shape, F32),
        vmem((2, lat_n, lon_n, feat), F32), vmem((2 * tok_n, feat), BF16), vmem((4 * (lat_n + lon_n), feat), BF16), vmem((tok_n, hid), F32),
        vmem((tok_n, hid), BF16), vmem((tok_n, feat), BF16), vmem((stations, feat), F32),
        vmem((stations, tok_n), BF16), vmem((tok_n, feat), F32), vmem((tok_n, feat), BF16),
        vmem((lat_n, lon_n, feat), F32),
        vmem((2, 4, 16, feat), BF16), vmem((2, 4, 16, feat), BF16),
        vmem((2, 4, 1, feat), F32), vmem((2, 4, 1, feat), F32),
        vmem((chunks, 4, 16, nbk), BF16), vmem((chunks, 4, 16, nbk), BF16),
        vmem((chunks, 4, 1, nbk), F32), vmem((chunks, 4, 1, nbk), F32),
        vmem((LANES, block_n), F32), vmem((nb, ns, LANES), F32), vmem((nb, ns, LANES), F32),
        vmem((ns, nb, LANES), F32), vmem((ns, nb, LANES), F32),
        vmem((2, LANES), F32), vmem((nb, 2, LANES), F32), vmem((ns, 2, LANES), F32),
        dma((10 + hid // nw,)), dma((2,)), dma((2,)), dma((2,)), dma((2, chunks)), dma((4,)), dma((4,)),
    ]
    sizes = (nb, ns, lat_n, lon_n, feat, hid, slot_n, tap_n, n1, n2, nbk, cw, nw)
    return pl.pallas_call(
        functools.partial(kernel, sizes),
        out_shape=pltpu.VMEM(base_state.shape, F32),
        in_specs=[pl.BlockSpec(memory_space=pl.ANY)] * 11,
        out_specs=pl.BlockSpec(memory_space=pltpu.VMEM),
        scratch_shapes=scratch,
        compiler_params=pltpu.CompilerParams(
            collective_id=0, has_side_effects=True, vmem_limit_bytes=56 * 2**20
        ),
    )(base_state, direction, residual, mix_coef, w_in, w_out, patch, count, pos, wgt, rinv)


def solution(mesh):
    return jax.shard_map(
        functools.partial(shards, mesh.shape["band"], mesh.shape["sector"]),
        mesh=mesh,
        in_specs=(
            P("band", "sector", None),
            P("band", "sector", None),
            P("band", "sector", None),
            P(),
            P(),
            P(),
            P(("band", "sector"), None, None),
            P(("band", "sector"), None),
            P(("band", "sector"), None, None, None),
            P(("band", "sector"), None, None, None),
            P(("band", "sector"), None, None),
        ),
        out_specs=P("band", "sector", None),
        check_vma=False,
    )
```

```python
import functools
import math

import jax
import jax.numpy as jnp
from jax import lax
from jax.experimental import pallas as pl
from jax.experimental.pallas import tpu as pltpu
from jax.sharding import PartitionSpec as P

MESH = pl.DeviceIdType.MESH
F32 = jnp.float32
BF16 = jnp.bfloat16
LANES = 128


def gelu_slope(preact):
    normal_cdf = 0.5 * (1.0 + lax.erf(preact * (1.0 / math.sqrt(2.0))))
    normal_pdf = jnp.exp(-0.5 * preact * preact) * (1.0 / math.sqrt(2.0 * math.pi))
    return normal_cdf + preact * normal_pdf


def nn(left, right):
    return jnp.dot(left, right, preferred_element_type=F32)


def nt(left, right):
    return lax.dot_general(left, right, (((1,), (1,)), ((), ())), preferred_element_type=F32)


def tn(left, right):
    return lax.dot_general(left, right, (((0,), (0,)), ((), ())), preferred_element_type=F32)


def fold_lanes(values):
    total = values[:, :LANES]
    for at in range(LANES, values.shape[1], LANES):
        total = total + values[:, at : at + LANES]
    return total


def shifted(part, lon_n):
    lon_at = lax.broadcasted_iota(jnp.int32, part[0].shape, 0)
    low = jnp.where(lon_at == 0, 0.0, pltpu.roll(part[0], 1, 0))
    high = jnp.where(lon_at == lon_n - 1, 0.0, pltpu.roll(part[2], lon_n - 1, 0))
    return low + part[1] + high


def inner_rows(row, coef, lat_n, lon_n):
    before, now = None, row(0)
    for i in range(lat_n):
        after = row(i + 1) if i < lat_n - 1 else None
        part = []
        for b in range(3):
            summed = coef[3 + b] * now
            if before is not None:
                summed = summed + coef[b] * before
            if after is not None:
                summed = summed + coef[6 + b] * after
            part.append(summed)
        yield shifted(part, lon_n)
        before, now = now, after


def rim_shares(north, south, west, east, corners, coef, lat_n, lon_n):
    lat_at = lax.broadcasted_iota(jnp.int32, (lat_n, west.shape[1]), 0)

    def column(mid, above, below, b):
        prev = jnp.where(lat_at == 0, above, pltpu.roll(mid, 1, 0))
        following = jnp.where(lat_at == lat_n - 1, below, pltpu.roll(mid, lat_n - 1, 0))
        return coef[b] * prev + coef[3 + b] * mid + coef[6 + b] * following

    rim_w = column(west, corners[0], corners[2], 0)
    rim_e = column(east, corners[1], corners[3], 2)
    first = shifted([coef[b] * north for b in range(3)], lon_n)
    last = shifted([coef[6 + b] * south for b in range(3)], lon_n)
    return first, last, rim_w, rim_e


def kernel(
    sizes,
    base_h, dir_h, res_h, coef_h, win_h, wout_h, patch_h, count_h, pos_h, wgt_h, rinv_h,
    out_ref,
    base, direc, res, coef, win, wout, patch, count, pos, wgt, rinv,
    acc, mixed, rimmed, slopes, hidden, tang, weights, onehot, obs, obs_b, gmix,
    fedge_s, fedge_r, fcorn_s, fcorn_r, bedge_s, bedge_r, bcorn_s, bcorn_r,
    pay, a0, a1, a2, a3, red0, red1, red2,
    load_sem, fs_sem, fr_sem, bs_sem, br_sem, ps_sem, pr_sem,
):
    nb, ns, lat_n, lon_n, feat, hid, slot_n, tap_n, n1, n2, nbk, cw, nw = sizes
    tok_n = lat_n * lon_n
    rim_n = 2 * (lat_n + lon_n)
    block_n = nb * ns
    last_i, last_j = lat_n - 1, lon_n - 1
    b = lax.axis_index("band")
    s = lax.axis_index("sector")

    def band(step):
        return lax.rem(b + step + nb, nb)

    def sector(step):
        return lax.rem(s + step + ns, ns)

    loads = {}
    pairs = dict(
        coef=(coef_h, coef), base=(base_h, base), dir=(dir_h, direc),
        patch=(patch_h, patch), count=(count_h, count), pos=(pos_h, pos), wgt=(wgt_h, wgt), rinv=(rinv_h, rinv),
    )
    for n in range(hid // nw):
        cols = pl.ds(n * nw, nw)
        pairs[n] = (win_h.at[:, cols], win.at[:, cols])
    later = dict(res=(res_h, res), wout=(wout_h, wout))

    def load(named):
        for name, (src, dst) in named.items():
            loads[name] = pltpu.make_async_copy(src, dst, load_sem.at[len(loads)])
            loads[name].start()

    load(pairs)

    edge_to = [(band(1), s), (band(-1), s), (b, sector(1)), (b, sector(-1))]
    corner_to = [
        (band(1), sector(1)), (band(1), sector(-1)), (band(-1), sector(1)), (band(-1), sector(-1)),
    ]
    partners = [(band(d), s) for d in range(1, nb)] + [(b, sector(d)) for d in range(1, ns)] + corner_to
    barrier = pltpu.get_barrier_semaphore()
    for partner in partners:
        pl.semaphore_signal(barrier, inc=1, device_id=partner, device_id_type=MESH)
    load(later)

    def send(src, dst, send_sem, recv_sem, to):
        copy = pltpu.make_async_remote_copy(
            src_ref=src, dst_ref=dst, send_sem=send_sem, recv_sem=recv_sem, device_id=to, device_id_type=MESH
        )
        copy.start()

    def landed(buffer, sem):
        pltpu.make_async_copy(buffer, buffer, sem).wait()

    loads["coef"].wait()
    loads["base"].wait()

    def premix(at, field, cols):
        taps = [coef[t : t + 1, cols] for t in range(9)]
        for i, summed in enumerate(inner_rows(lambda r: field[r, :, cols], taps, lat_n, lon_n)):
            start = at * tok_n + i * lon_n
            mixed[start : start + lon_n, cols] = summed.astype(BF16)
            acc[at, i, :, cols] = summed

    def premix_base(k, carry):
        premix(0, base, pl.ds(pl.multiple_of(k * cw, cw), cw))
        return carry

    lax.fori_loop(0, feat // cw, premix_base, 0)

    loads["dir"].wait()
    rim_at = ((last_i, last_j), (last_i, 0), (0, last_j), (0, 0))
    for at, field in enumerate((base, direc)):
        for side, rim in enumerate((field[last_i], field[0], field[:, last_j], field[:, 0])):
            fedge_s[side, at] = rim.astype(BF16)
        for side, (ci, cj) in enumerate(rim_at):
            fcorn_s[side, at] = field[ci, cj : cj + 1]
    pl.semaphore_wait(barrier, len(partners))
    for side in range(4):
        send(fcorn_s.at[side], fcorn_r.at[side], fs_sem.at[1], fr_sem.at[1], corner_to[side])
    for side in (2, 3, 0, 1):
        send(fedge_s.at[side], fedge_r.at[side], fs_sem.at[0], fr_sem.at[0], edge_to[side])

    for name in ("patch", "count", "pos", "wgt", "rinv"):
        loads[name].wait()
    slot_at = lax.broadcasted_iota(jnp.int32, (slot_n, block_n), 0)
    tap_all = slot_n * tap_n
    pay[...] = jnp.zeros_like(pay)
    pay[0:slot_n] = patch[...].astype(F32)
    pay[slot_n : 2 * slot_n] = jnp.where(slot_at < count[...], rinv[...], 0.0)
    pay[2 * slot_n : 2 * slot_n + tap_all] = pos[...].astype(F32)
    pay[2 * slot_n + tap_all : 2 * slot_n + 2 * tap_all] = wgt[...]
    a0[...] = jnp.transpose(pay[...]).reshape(nb, ns, LANES)

    a1[b] = a0[b]
    for d in range(1, nb):
        send(a0.at[band(d)], a1.at[b], ps_sem.at[0], pr_sem.at[0], (band(d), s))

    inside_n = (b > 0).astype(F32)
    inside_s = (b < nb - 1).astype(F32)

    def rims_in(edge, corn, taps, cols):
        corners = [corn.at[side][:, cols] * (inside_n if side < 2 else inside_s) for side in range(4)]
        north = edge.at[0][:, cols].astype(F32) * inside_n
        south = edge.at[1][:, cols].astype(F32) * inside_s
        west = edge.at[2][:, cols].astype(F32)
        east = edge.at[3][:, cols].astype(F32)
        return rim_shares(north, south, west, east, corners, taps, lat_n, lon_n)

    steps = hid // n1
    parts = feat // cw
    share = -(-parts // steps)
    for n in range(steps):
        if n * n1 % nw == 0:
            loads[n * n1 // nw].wait()
        cols = slice(n * n1, (n + 1) * n1)
        slopes[:, cols] = gelu_slope(nn(mixed[:tok_n], win[:, cols]))
        for k in range(n * share, min((n + 1) * share, parts)):
            premix(1, direc, slice(k * cw, (k + 1) * cw))
    for n in range(steps):
        cols = slice(n * n1, (n + 1) * n1)
        hidden[:, cols] = (slopes[:, cols] * nn(mixed[tok_n:], win[:, cols])).astype(BF16)
        if n == steps // 3:
            landed(a1.at[pl.ds(0, nb - 1)], pr_sem.at[0])
            for q in range(ns):
                a2[q] = a1[:, q, :]
            a3[s] = a2[s]
            for d in range(1, ns):
                send(a2.at[sector(d)], a3.at[s], ps_sem.at[1], pr_sem.at[1], (b, sector(d)))

    loads["res"].wait()
    zero = jnp.zeros((lon_n, LANES), F32)

    def square(i, carry):
        norm, grow = carry
        r, d = res[i], direc[i]
        return norm + fold_lanes(r * r), grow + fold_lanes(d * d)

    norm, grow = lax.fori_loop(0, lat_n, square, (zero, zero))
    red0[0:1] = jnp.sum(norm, axis=0, keepdims=True)
    red0[1:2] = jnp.sum(grow, axis=0, keepdims=True)

    landed(fedge_r, fr_sem.at[0])
    landed(fcorn_r, fr_sem.at[1])

    for k in range(feat // nbk):
        cols = slice(k * nbk, (k + 1) * nbk)
        taps = [coef[t : t + 1, cols] for t in range(9)]
        for at in range(2):
            first, last, rim_w, rim_e = rims_in(fedge_r.at[:, at], fcorn_r.at[:, at], taps, cols)
            lon_at = lax.broadcasted_iota(jnp.int32, first.shape, 0)
            rows = [acc[at, :, 0, cols] + rim_w, acc[at, :, last_j, cols] + rim_e]
            for i, share in ((0, first), (last_i, last)):
                row = acc[at, i, :, cols] + share
                row = jnp.where(lon_at == 0, row + rim_w[i : i + 1], row)
                rows.insert(-2, jnp.where(lon_at == last_j, row + rim_e[i : i + 1], row))
            start = at * rim_n
            for row in rows:
                rimmed[start : start + row.shape[0], cols] = row.astype(BF16)
                start += row.shape[0]
    lon_at = lax.broadcasted_iota(jnp.int32, (lon_n, n1), 0)
    for n in range(steps):
        cols = slice(n * n1, (n + 1) * n1)
        both = nn(rimmed[...], win[:, cols])
        slope = gelu_slope(both[:rim_n])
        value = slope * both[rim_n:]
        slopes[:lon_n, cols] = slope[:lon_n]
        slopes[last_i * lon_n :, cols] = slope[lon_n : 2 * lon_n]
        hidden[:lon_n, cols] = value[:lon_n].astype(BF16)
        hidden[last_i * lon_n :, cols] = value[lon_n : 2 * lon_n].astype(BF16)
        at_w, at_e = 2 * lon_n, 2 * lon_n + lat_n
        for i in range(1, last_i):
            start = i * lon_n
            slopes[start : start + 1, cols] = slope[at_w + i : at_w + i + 1]
            slopes[start + last_j : start + lon_n, cols] = slope[at_e + i : at_e + i + 1]
            inner = hidden[start : start + lon_n, cols].astype(F32)
            inner = jnp.where(lon_at == 0, value[at_w + i : at_w + i + 1], inner)
            inner = jnp.where(lon_at == last_j, value[at_e + i : at_e + i + 1], inner)
            hidden[start : start + lon_n, cols] = inner.astype(BF16)

    stations = slot_n * block_n
    rb = min(32, block_n)
    blocks = [(c, r) for c in range(slot_n) for r in range(0, block_n, rb)]

    def place(c):
        told = a3[...].reshape(block_n, LANES)
        cell_at = lax.broadcasted_iota(jnp.int32, (block_n, tok_n), 1).astype(F32)
        onehot[c * block_n : (c + 1) * block_n] = jnp.where(told[:, c : c + 1] == cell_at, 1.0, 0.0).astype(BF16)

    def spread(c, r):
        rows = a3[r // nb : (r + rb) // nb].reshape(rb, LANES)
        lane_at = lax.broadcasted_iota(jnp.int32, (rb, LANES), 1).astype(F32)
        first = 2 * slot_n + c * tap_n
        chans = [jnp.broadcast_to(rows[:, first + k : first + k + 1], (rb, LANES)) for k in range(tap_n)]
        first += tap_all
        wgts = [jnp.broadcast_to(rows[:, first + k : first + k + 1], (rb, LANES)) for k in range(tap_n)]
        for j in range(feat // LANES):
            here = lane_at + float(j * LANES)
            summed = jnp.where(chans[0] == here, wgts[0], 0.0)
            for k in range(1, tap_n):
                summed = summed + jnp.where(chans[k] == here, wgts[k], 0.0)
            weights[c * block_n + r : c * block_n + r + rb, j * LANES : (j + 1) * LANES] = summed

    seen = jnp.zeros((stations, LANES), F32)
    loads["wout"].wait()
    for n in range(feat // n2):
        cols = slice(n * n2, (n + 1) * n2)
        own = direc[:, :, cols].reshape(tok_n, n2)
        tang[:, cols] = (own + nn(hidden[...], wout[:, cols])).astype(BF16)
        if n == max(feat // n2 - 2, 0):
            landed(a3.at[pl.ds(0, ns - 1)], pr_sem.at[1])
    for c, r in blocks:
        spread(c, r)
    for c in range(slot_n):
        place(c)
    for n in range(feat // n2):
        cols = slice(n * n2, (n + 1) * n2)
        sampled = nn(onehot[...], tang[:, cols])
        seen = seen + fold_lanes(sampled * weights[:, cols])
    misfit = jnp.sum(seen, axis=1, keepdims=True)
    told = a3[...].reshape(block_n, LANES)
    inverse = jnp.concatenate([told[:, slot_n + c : slot_n + c + 1] for c in range(slot_n)], axis=0)
    scaled = inverse * misfit
    lane0 = lax.broadcasted_iota(jnp.int32, (1, LANES), 1) == 0
    red0[1:2] = red0[1:2] + jnp.where(lane0, jnp.sum(scaled * misfit, axis=0, keepdims=True), 0.0)

    red1[b] = red0[...]
    for d in range(1, nb):
        send(red0, red1.at[b], ps_sem.at[2], pr_sem.at[2], (band(d), s))

    for n in range(feat // n2):
        cols = slice(n * n2, (n + 1) * n2)
        summed = tn(onehot[...], (scaled * weights[:, cols]).astype(BF16))
        obs[:, cols] = summed
        obs_b[:, cols] = summed.astype(BF16)

    for n in range(hid // n1):
        rows = slice(n * n1, (n + 1) * n1)
        hidden[:, rows] = (slopes[:, rows] * nt(obs_b[...], wout[rows, :])).astype(BF16)

    for n in range(feat // nbk):
        rows = slice(n * nbk, (n + 1) * nbk)
        part = nt(hidden[...], win[rows, :]).reshape(lat_n, lon_n, nbk)
        gmix[:, :, rows] = part
        for side, rim in enumerate(
            (gmix[last_i, :, rows], gmix[0, :, rows], gmix[:, last_j, rows], gmix[:, 0, rows])
        ):
            bedge_s[side, :, rows] = rim.astype(BF16)
        for side, (ci, cj) in enumerate(rim_at):
            bcorn_s[side, :, rows] = gmix[ci, cj : cj + 1, rows]
        if n == 1:
            landed(red1.at[pl.ds(0, nb - 1)], pr_sem.at[2])
            total = red1[0]
            for d in range(1, nb):
                total = total + red1[d]
            red2[s] = total
            for d in range(1, ns):
                send(red2.at[s], red2.at[s], ps_sem.at[3], pr_sem.at[3], (b, sector(d)))

    for side in range(4):
        send(bcorn_s.at[side], bcorn_r.at[side], bs_sem.at[1], br_sem.at[1], corner_to[side])
    for side in (2, 3, 0, 1):
        send(bedge_s.at[side], bedge_r.at[side], bs_sem.at[0], br_sem.at[0], edge_to[side])

    def preunmix(k, carry):
        cols = pl.ds(pl.multiple_of(k * cw, cw), cw)
        taps = [coef[8 - t : 9 - t, cols] for t in range(9)]
        for i, summed in enumerate(inner_rows(lambda r: gmix[r, :, cols], taps, lat_n, lon_n)):
            acc[0, i, :, cols] = direc[i, :, cols] + obs[i * lon_n : (i + 1) * lon_n, cols] + summed
        return carry

    lax.fori_loop(0, feat // cw, preunmix, 0)

    landed(red2.at[pl.ds(0, ns - 1)], pr_sem.at[3])
    total = red2[0]
    for d in range(1, ns):
        total = total + red2[d]
    total = jnp.sum(total, axis=1, keepdims=True)
    alpha = total[0:1] / total[1:2]

    landed(bedge_r, br_sem.at[0])
    landed(bcorn_r, br_sem.at[1])

    def unmix(k, carry):
        cols = pl.ds(pl.multiple_of(k * cw, cw), cw)
        taps = [coef[8 - t : 9 - t, cols] for t in range(9)]
        first, last, rim_w, rim_e = rims_in(bedge_r, bcorn_r, taps, cols)
        lon_at = lax.broadcasted_iota(jnp.int32, first.shape, 0)
        for i in range(lat_n):
            rim = jnp.where(lon_at == 0, rim_w[i : i + 1], 0.0) + jnp.where(lon_at == last_j, rim_e[i : i + 1], 0.0)
            if i == 0:
                rim = rim + first
            if i == last_i:
                rim = rim + last
            out_ref[i, :, cols] = res[i, :, cols] - alpha * (acc[0, i, :, cols] + rim)
        return carry

    lax.fori_loop(0, feat // cw, unmix, 0)

    landed(fedge_s, fs_sem.at[0])
    landed(fcorn_s, fs_sem.at[1])
    landed(bedge_s, bs_sem.at[0])
    landed(bcorn_s, bs_sem.at[1])
    landed(a1.at[pl.ds(0, nb - 1)], ps_sem.at[0])
    landed(a3.at[pl.ds(0, ns - 1)], ps_sem.at[1])
    landed(red1.at[pl.ds(0, nb - 1)], ps_sem.at[2])
    landed(red2.at[pl.ds(0, ns - 1)], ps_sem.at[3])


def shards(
    nb, ns,
    base_state, direction, residual, mix_coef, w_in, w_out,
    obs_patch, obs_count, obs_pos, obs_wgt, obs_rinv,
):
    lat_n, lon_n, feat = base_state.shape
    hid = w_in.shape[1]
    slot_n, tap_n = obs_pos.shape[2:]
    tok_n = lat_n * lon_n
    block_n = nb * ns
    n1 = min(512, hid)
    n2 = min(512, feat)
    nbk = min(512, feat)
    patch = obs_patch[0].T
    count = obs_count
    pos = jnp.transpose(obs_pos[0], (1, 2, 0)).reshape(slot_n * tap_n, block_n)
    wgt = jnp.transpose(obs_wgt[0], (1, 2, 0)).reshape(slot_n * tap_n, block_n)
    rinv = obs_rinv[0].T
    stations = slot_n * block_n
    dma = pltpu.SemaphoreType.DMA
    vmem = pltpu.VMEM
    cw = min(256, nbk)
    nw = 2 * n1 if hid % (2 * n1) == 0 else n1
    scratch = [
        vmem((lat_n, lon_n, feat), F32), vmem((lat_n, lon_n, feat), F32), vmem((lat_n, lon_n, feat), F32),
        vmem(mix_coef.shape, F32), vmem(w_in.shape, BF16), vmem(w_out.shape, BF16),
        vmem(patch.shape, jnp.int32), vmem(count.shape, jnp.int32), vmem(pos.shape, jnp.int32),
        vmem(wgt.shape, F32), vmem(rinv.shape, F32),
        vmem((2, lat_n, lon_n, feat), F32), vmem((2 * tok_n, feat), BF16), vmem((4 * (lat_n + lon_n), feat), BF16), vmem((tok_n, hid), F32),
        vmem((tok_n, hid), BF16), vmem((tok_n, feat), BF16), vmem((stations, feat), F32),
        vmem((stations, tok_n), BF16), vmem((tok_n, feat), F32), vmem((tok_n, feat), BF16),
        vmem((lat_n, lon_n, feat), F32),
        vmem((4, 2, 16, feat), BF16), vmem((4, 2, 16, feat), BF16),
        vmem((4, 2, 1, feat), F32), vmem((4, 2, 1, feat), F32),
        vmem((4, 16, feat), BF16), vmem((4, 16, feat), BF16),
        vmem((4, 1, feat), F32), vmem((4, 1, feat), F32),
        vmem((LANES, block_n), F32), vmem((nb, ns, LANES), F32), vmem((nb, ns, LANES), F32),
        vmem((ns, nb, LANES), F32), vmem((ns, nb, LANES), F32),
        vmem((2, LANES), F32), vmem((nb, 2, LANES), F32), vmem((ns, 2, LANES), F32),
        dma((10 + hid // nw,)), dma((2,)), dma((2,)), dma((2,)), dma((2,)), dma((4,)), dma((4,)),
    ]
    sizes = (nb, ns, lat_n, lon_n, feat, hid, slot_n, tap_n, n1, n2, nbk, cw, nw)
    return pl.pallas_call(
        functools.partial(kernel, sizes),
        out_shape=pltpu.VMEM(base_state.shape, F32),
        in_specs=[pl.BlockSpec(memory_space=pl.ANY)] * 11,
        out_specs=pl.BlockSpec(memory_space=pltpu.VMEM),
        scratch_shapes=scratch,
        compiler_params=pltpu.CompilerParams(
            collective_id=0, has_side_effects=True, vmem_limit_bytes=56 * 2**20
        ),
    )(base_state, direction, residual, mix_coef, w_in, w_out, patch, count, pos, wgt, rinv)


def solution(mesh):
    return jax.shard_map(
        functools.partial(shards, mesh.shape["band"], mesh.shape["sector"]),
        mesh=mesh,
        in_specs=(
            P("band", "sector", None),
            P("band", "sector", None),
            P("band", "sector", None),
            P(),
            P(),
            P(),
            P(("band", "sector"), None, None),
            P(("band", "sector"), None),
            P(("band", "sector"), None, None, None),
            P(("band", "sector"), None, None, None),
            P(("band", "sector"), None, None),
        ),
        out_specs=P("band", "sector", None),
        check_vma=False,
    )
```

```python
import functools
import math

import jax
import jax.numpy as jnp
from jax import lax
from jax.experimental import pallas as pl
from jax.experimental.pallas import tpu as pltpu
from jax.sharding import PartitionSpec as P

MESH = pl.DeviceIdType.MESH
F32 = jnp.float32
BF16 = jnp.bfloat16
LANES = 128


def gelu_slope(preact):
    normal_cdf = 0.5 * (1.0 + lax.erf(preact * (1.0 / math.sqrt(2.0))))
    normal_pdf = jnp.exp(-0.5 * preact * preact) * (1.0 / math.sqrt(2.0 * math.pi))
    return normal_cdf + preact * normal_pdf


def nn(left, right):
    return jnp.dot(left, right, preferred_element_type=F32)


def nt(left, right):
    return lax.dot_general(left, right, (((1,), (1,)), ((), ())), preferred_element_type=F32)


def tn(left, right):
    return lax.dot_general(left, right, (((0,), (0,)), ((), ())), preferred_element_type=F32)


def fold_lanes(values):
    total = values[:, :LANES]
    for at in range(LANES, values.shape[1], LANES):
        total = total + values[:, at : at + LANES]
    return total


def shifted(part, lon_n):
    lon_at = lax.broadcasted_iota(jnp.int32, part[0].shape, 0)
    low = jnp.where(lon_at == 0, 0.0, pltpu.roll(part[0], 1, 0))
    high = jnp.where(lon_at == lon_n - 1, 0.0, pltpu.roll(part[2], lon_n - 1, 0))
    return low + part[1] + high


def inner_rows(row, coef, lat_n, lon_n):
    before, now = None, row(0)
    for i in range(lat_n):
        after = row(i + 1) if i < lat_n - 1 else None
        part = []
        for b in range(3):
            summed = coef[3 + b] * now
            if before is not None:
                summed = summed + coef[b] * before
            if after is not None:
                summed = summed + coef[6 + b] * after
            part.append(summed)
        yield shifted(part, lon_n)
        before, now = now, after


def rim_shares(north, south, west, east, corners, coef, lat_n, lon_n):
    lat_at = lax.broadcasted_iota(jnp.int32, (lat_n, west.shape[1]), 0)

    def column(mid, above, below, b):
        prev = jnp.where(lat_at == 0, above, pltpu.roll(mid, 1, 0))
        following = jnp.where(lat_at == lat_n - 1, below, pltpu.roll(mid, lat_n - 1, 0))
        return coef[b] * prev + coef[3 + b] * mid + coef[6 + b] * following

    rim_w = column(west, corners[0], corners[2], 0)
    rim_e = column(east, corners[1], corners[3], 2)
    first = shifted([coef[b] * north for b in range(3)], lon_n)
    last = shifted([coef[6 + b] * south for b in range(3)], lon_n)
    return first, last, rim_w, rim_e


def kernel(
    sizes,
    base_h, dir_h, res_h, coef_h, win_h, wout_h, patch_h, count_h, pos_h, wgt_h, rinv_h,
    out_ref,
    base, direc, res, coef, win, wout, patch, count, pos, wgt, rinv,
    acc, mixed, rimmed, slopes, hidden, tang, weights, onehot, obs, obs_b, gmix,
    fedge_s, fedge_r, fcorn_s, fcorn_r, bedge_s, bedge_r, bcorn_s, bcorn_r,
    pay, a0, a1, a2, a3, red0, red1, red2,
    load_sem, fs_sem, fr_sem, bs_sem, br_sem, ps_sem, pr_sem,
):
    nb, ns, lat_n, lon_n, feat, hid, slot_n, tap_n, n1, n2, nbk, cw, nw = sizes
    tok_n = lat_n * lon_n
    rim_n = 2 * (lat_n + lon_n)
    block_n = nb * ns
    last_i, last_j = lat_n - 1, lon_n - 1
    b = lax.axis_index("band")
    s = lax.axis_index("sector")

    def band(step):
        return lax.rem(b + step + nb, nb)

    def sector(step):
        return lax.rem(s + step + ns, ns)

    loads = {}
    pairs = dict(
        coef=(coef_h, coef), base=(base_h, base), dir=(dir_h, direc),
        patch=(patch_h, patch), count=(count_h, count), pos=(pos_h, pos), wgt=(wgt_h, wgt), rinv=(rinv_h, rinv),
    )
    for n in range(hid // nw):
        cols = pl.ds(n * nw, nw)
        pairs[n] = (win_h.at[:, cols], win.at[:, cols])
    later = dict(res=(res_h, res), wout=(wout_h, wout))

    def load(named):
        for name, (src, dst) in named.items():
            loads[name] = pltpu.make_async_copy(src, dst, load_sem.at[len(loads)])
            loads[name].start()

    load(pairs)

    edge_to = [(band(1), s), (band(-1), s), (b, sector(1)), (b, sector(-1))]
    corner_to = [
        (band(1), sector(1)), (band(1), sector(-1)), (band(-1), sector(1)), (band(-1), sector(-1)),
    ]
    partners = [(band(d), s) for d in range(1, nb)] + [(b, sector(d)) for d in range(1, ns)] + corner_to
    barrier = pltpu.get_barrier_semaphore()
    for partner in partners:
        pl.semaphore_signal(barrier, inc=1, device_id=partner, device_id_type=MESH)
    load(later)

    def send(src, dst, send_sem, recv_sem, to):
        copy = pltpu.make_async_remote_copy(
            src_ref=src, dst_ref=dst, send_sem=send_sem, recv_sem=recv_sem, device_id=to, device_id_type=MESH
        )
        copy.start()

    def landed(buffer, sem):
        pltpu.make_async_copy(buffer, buffer, sem).wait()

    loads["coef"].wait()
    loads["base"].wait()

    def premix(at, field, cols):
        taps = [coef[t : t + 1, cols] for t in range(9)]
        for i, summed in enumerate(inner_rows(lambda r: field[r, :, cols], taps, lat_n, lon_n)):
            start = at * tok_n + i * lon_n
            mixed[start : start + lon_n, cols] = summed.astype(BF16)
            acc[at, i, :, cols] = summed

    def premix_base(k, carry):
        premix(0, base, pl.ds(pl.multiple_of(k * cw, cw), cw))
        return carry

    lax.fori_loop(0, feat // cw, premix_base, 0)

    loads["dir"].wait()
    rim_at = ((last_i, last_j), (last_i, 0), (0, last_j), (0, 0))
    for at, field in enumerate((base, direc)):
        for side, rim in enumerate((field[last_i], field[0], field[:, last_j], field[:, 0])):
            fedge_s[side, at] = rim.astype(BF16)
        for side, (ci, cj) in enumerate(rim_at):
            fcorn_s[side, at] = field[ci, cj : cj + 1]
    pl.semaphore_wait(barrier, len(partners))
    for side in range(4):
        send(fcorn_s.at[side], fcorn_r.at[side], fs_sem.at[1], fr_sem.at[1], corner_to[side])
    for side in (2, 3, 0, 1):
        send(fedge_s.at[side], fedge_r.at[side], fs_sem.at[0], fr_sem.at[0], edge_to[side])

    for name in ("patch", "count", "pos", "wgt", "rinv"):
        loads[name].wait()
    slot_at = lax.broadcasted_iota(jnp.int32, (slot_n, block_n), 0)
    tap_all = slot_n * tap_n
    pay[...] = jnp.zeros_like(pay)
    pay[0:slot_n] = patch[...].astype(F32)
    pay[slot_n : 2 * slot_n] = jnp.where(slot_at < count[...], rinv[...], 0.0)
    pay[2 * slot_n : 2 * slot_n + tap_all] = pos[...].astype(F32)
    pay[2 * slot_n + tap_all : 2 * slot_n + 2 * tap_all] = wgt[...]
    a0[...] = jnp.transpose(pay[...]).reshape(nb, ns, LANES)

    a1[b] = a0[b]
    for d in range(1, nb):
        send(a0.at[band(d)], a1.at[b], ps_sem.at[0], pr_sem.at[0], (band(d), s))

    inside_n = (b > 0).astype(F32)
    inside_s = (b < nb - 1).astype(F32)

    def rims_in(edge, corn, taps, cols):
        corners = [corn.at[side][:, cols] * (inside_n if side < 2 else inside_s) for side in range(4)]
        north = edge.at[0][:, cols].astype(F32) * inside_n
        south = edge.at[1][:, cols].astype(F32) * inside_s
        west = edge.at[2][:, cols].astype(F32)
        east = edge.at[3][:, cols].astype(F32)
        return rim_shares(north, south, west, east, corners, taps, lat_n, lon_n)

    steps = hid // n1
    parts = feat // cw
    share = -(-parts // steps)
    for n in range(steps):
        if n * n1 % nw == 0:
            loads[n * n1 // nw].wait()
        cols = slice(n * n1, (n + 1) * n1)
        slopes[:, cols] = gelu_slope(nn(mixed[:tok_n], win[:, cols]))
        for k in range(n * share, min((n + 1) * share, parts)):
            premix(1, direc, slice(k * cw, (k + 1) * cw))
    for n in range(steps):
        cols = slice(n * n1, (n + 1) * n1)
        hidden[:, cols] = (slopes[:, cols] * nn(mixed[tok_n:], win[:, cols])).astype(BF16)
        if n == steps // 3:
            landed(a1.at[pl.ds(0, nb - 1)], pr_sem.at[0])
            for q in range(ns):
                a2[q] = a1[:, q, :]
            a3[s] = a2[s]
            for d in range(1, ns):
                send(a2.at[sector(d)], a3.at[s], ps_sem.at[1], pr_sem.at[1], (b, sector(d)))

    loads["res"].wait()
    zero = jnp.zeros((lon_n, LANES), F32)

    def square(i, carry):
        norm, grow = carry
        r, d = res[i], direc[i]
        return norm + fold_lanes(r * r), grow + fold_lanes(d * d)

    norm, grow = lax.fori_loop(0, lat_n, square, (zero, zero))
    red0[0:1] = jnp.sum(norm, axis=0, keepdims=True)
    red0[1:2] = jnp.sum(grow, axis=0, keepdims=True)

    landed(fedge_r, fr_sem.at[0])
    landed(fcorn_r, fr_sem.at[1])

    for k in range(feat // nbk):
        cols = slice(k * nbk, (k + 1) * nbk)
        taps = [coef[t : t + 1, cols] for t in range(9)]
        for at in range(2):
            first, last, rim_w, rim_e = rims_in(fedge_r.at[:, at], fcorn_r.at[:, at], taps, cols)
            lon_at = lax.broadcasted_iota(jnp.int32, first.shape, 0)
            rows = [acc[at, :, 0, cols] + rim_w, acc[at, :, last_j, cols] + rim_e]
            for i, share in ((0, first), (last_i, last)):
                row = acc[at, i, :, cols] + share
                row = jnp.where(lon_at == 0, row + rim_w[i : i + 1], row)
                rows.insert(-2, jnp.where(lon_at == last_j, row + rim_e[i : i + 1], row))
            start = at * rim_n
            for row in rows:
                rimmed[start : start + row.shape[0], cols] = row.astype(BF16)
                start += row.shape[0]
    lon_at = lax.broadcasted_iota(jnp.int32, (lon_n, n1), 0)
    for n in range(steps):
        cols = slice(n * n1, (n + 1) * n1)
        both = nn(rimmed[...], win[:, cols])
        slope = gelu_slope(both[:rim_n])
        value = slope * both[rim_n:]
        slopes[:lon_n, cols] = slope[:lon_n]
        slopes[last_i * lon_n :, cols] = slope[lon_n : 2 * lon_n]
        hidden[:lon_n, cols] = value[:lon_n].astype(BF16)
        hidden[last_i * lon_n :, cols] = value[lon_n : 2 * lon_n].astype(BF16)
        at_w, at_e = 2 * lon_n, 2 * lon_n + lat_n
        for i in range(1, last_i):
            start = i * lon_n
            slopes[start : start + 1, cols] = slope[at_w + i : at_w + i + 1]
            slopes[start + last_j : start + lon_n, cols] = slope[at_e + i : at_e + i + 1]
            inner = hidden[start : start + lon_n, cols].astype(F32)
            inner = jnp.where(lon_at == 0, value[at_w + i : at_w + i + 1], inner)
            inner = jnp.where(lon_at == last_j, value[at_e + i : at_e + i + 1], inner)
            hidden[start : start + lon_n, cols] = inner.astype(BF16)

    stations = slot_n * block_n
    rb = min(32, block_n)
    blocks = [(c, r) for c in range(slot_n) for r in range(0, block_n, rb)]

    def place(c):
        told = a3[...].reshape(block_n, LANES)
        cell_at = lax.broadcasted_iota(jnp.int32, (block_n, tok_n), 1).astype(F32)
        onehot[c * block_n : (c + 1) * block_n] = jnp.where(told[:, c : c + 1] == cell_at, 1.0, 0.0).astype(BF16)

    def spread(c, r):
        rows = a3[r // nb : (r + rb) // nb].reshape(rb, LANES)
        lane_at = lax.broadcasted_iota(jnp.int32, (rb, LANES), 1).astype(F32)
        first = 2 * slot_n + c * tap_n
        chans = [jnp.broadcast_to(rows[:, first + k : first + k + 1], (rb, LANES)) for k in range(tap_n)]
        first += tap_all
        wgts = [jnp.broadcast_to(rows[:, first + k : first + k + 1], (rb, LANES)) for k in range(tap_n)]
        for j in range(feat // LANES):
            here = lane_at + float(j * LANES)
            summed = jnp.where(chans[0] == here, wgts[0], 0.0)
            for k in range(1, tap_n):
                summed = summed + jnp.where(chans[k] == here, wgts[k], 0.0)
            weights[c * block_n + r : c * block_n + r + rb, j * LANES : (j + 1) * LANES] = summed

    seen = jnp.zeros((stations, LANES), F32)
    loads["wout"].wait()
    for n in range(feat // n2):
        cols = slice(n * n2, (n + 1) * n2)
        own = direc[:, :, cols].reshape(tok_n, n2)
        tang[:, cols] = (own + nn(hidden[...], wout[:, cols])).astype(BF16)
        if n == max(feat // n2 - 2, 0):
            landed(a3.at[pl.ds(0, ns - 1)], pr_sem.at[1])
    for c, r in blocks:
        spread(c, r)
    for c in range(slot_n):
        place(c)
    for n in range(feat // n2):
        cols = slice(n * n2, (n + 1) * n2)
        sampled = nn(onehot[...], tang[:, cols])
        seen = seen + fold_lanes(sampled * weights[:, cols])
    misfit = jnp.sum(seen, axis=1, keepdims=True)
    told = a3[...].reshape(block_n, LANES)
    inverse = jnp.concatenate([told[:, slot_n + c : slot_n + c + 1] for c in range(slot_n)], axis=0)
    scaled = inverse * misfit
    lane0 = lax.broadcasted_iota(jnp.int32, (1, LANES), 1) == 0
    red0[1:2] = red0[1:2] + jnp.where(lane0, jnp.sum(scaled * misfit, axis=0, keepdims=True), 0.0)

    red1[b] = red0[...]
    for d in range(1, nb):
        send(red0, red1.at[b], ps_sem.at[2], pr_sem.at[2], (band(d), s))

    for n in range(feat // n2):
        cols = slice(n * n2, (n + 1) * n2)
        summed = tn(onehot[...], (scaled * weights[:, cols]).astype(BF16))
        obs[:, cols] = summed
        obs_b[:, cols] = summed.astype(BF16)

    for n in range(hid // n1):
        rows = slice(n * n1, (n + 1) * n1)
        hidden[:, rows] = (slopes[:, rows] * nt(obs_b[...], wout[rows, :])).astype(BF16)

    for n in range(feat // nbk):
        rows = slice(n * nbk, (n + 1) * nbk)
        part = nt(hidden[...], win[rows, :]).reshape(lat_n, lon_n, nbk)
        gmix[:, :, rows] = part
        for side, rim in enumerate(
            (gmix[last_i, :, rows], gmix[0, :, rows], gmix[:, last_j, rows], gmix[:, 0, rows])
        ):
            bedge_s[side, :, rows] = rim.astype(BF16)
        for side, (ci, cj) in enumerate(rim_at):
            bcorn_s[side, :, rows] = gmix[ci, cj : cj + 1, rows]

    for side in range(4):
        send(bcorn_s.at[side], bcorn_r.at[side], bs_sem.at[1], br_sem.at[1], corner_to[side])
    for side in (2, 3, 0, 1):
        send(bedge_s.at[side], bedge_r.at[side], bs_sem.at[0], br_sem.at[0], edge_to[side])

    landed(red1.at[pl.ds(0, nb - 1)], pr_sem.at[2])
    total = red1[0]
    for d in range(1, nb):
        total = total + red1[d]
    red2[s] = total
    for d in range(1, ns):
        send(red2.at[s], red2.at[s], ps_sem.at[3], pr_sem.at[3], (b, sector(d)))

    def preunmix(k, carry):
        cols = pl.ds(pl.multiple_of(k * cw, cw), cw)
        taps = [coef[8 - t : 9 - t, cols] for t in range(9)]
        for i, summed in enumerate(inner_rows(lambda r: gmix[r, :, cols], taps, lat_n, lon_n)):
            acc[0, i, :, cols] = direc[i, :, cols] + obs[i * lon_n : (i + 1) * lon_n, cols] + summed
        return carry

    lax.fori_loop(0, feat // cw, preunmix, 0)

    landed(red2.at[pl.ds(0, ns - 1)], pr_sem.at[3])
    total = red2[0]
    for d in range(1, ns):
        total = total + red2[d]
    total = jnp.sum(total, axis=1, keepdims=True)
    alpha = total[0:1] / total[1:2]

    landed(bedge_r, br_sem.at[0])
    landed(bcorn_r, br_sem.at[1])

    def unmix(k, carry):
        cols = pl.ds(pl.multiple_of(k * cw, cw), cw)
        taps = [coef[8 - t : 9 - t, cols] for t in range(9)]
        first, last, rim_w, rim_e = rims_in(bedge_r, bcorn_r, taps, cols)
        lon_at = lax.broadcasted_iota(jnp.int32, first.shape, 0)
        for i in range(lat_n):
            rim = jnp.where(lon_at == 0, rim_w[i : i + 1], 0.0) + jnp.where(lon_at == last_j, rim_e[i : i + 1], 0.0)
            if i == 0:
                rim = rim + first
            if i == last_i:
                rim = rim + last
            out_ref[i, :, cols] = res[i, :, cols] - alpha * (acc[0, i, :, cols] + rim)
        return carry

    lax.fori_loop(0, feat // cw, unmix, 0)

    landed(fedge_s, fs_sem.at[0])
    landed(fcorn_s, fs_sem.at[1])
    landed(bedge_s, bs_sem.at[0])
    landed(bcorn_s, bs_sem.at[1])
    landed(a1.at[pl.ds(0, nb - 1)], ps_sem.at[0])
    landed(a3.at[pl.ds(0, ns - 1)], ps_sem.at[1])
    landed(red1.at[pl.ds(0, nb - 1)], ps_sem.at[2])
    landed(red2.at[pl.ds(0, ns - 1)], ps_sem.at[3])


def shards(
    nb, ns,
    base_state, direction, residual, mix_coef, w_in, w_out,
    obs_patch, obs_count, obs_pos, obs_wgt, obs_rinv,
):
    lat_n, lon_n, feat = base_state.shape
    hid = w_in.shape[1]
    slot_n, tap_n = obs_pos.shape[2:]
    tok_n = lat_n * lon_n
    block_n = nb * ns
    n1 = min(512, hid)
    n2 = min(512, feat)
    nbk = min(512, feat)
    patch = obs_patch[0].T
    count = obs_count
    pos = jnp.transpose(obs_pos[0], (1, 2, 0)).reshape(slot_n * tap_n, block_n)
    wgt = jnp.transpose(obs_wgt[0], (1, 2, 0)).reshape(slot_n * tap_n, block_n)
    rinv = obs_rinv[0].T
    stations = slot_n * block_n
    dma = pltpu.SemaphoreType.DMA
    vmem = pltpu.VMEM
    cw = min(256, nbk)
    nw = 2 * n1 if hid % (2 * n1) == 0 else n1
    scratch = [
        vmem((lat_n, lon_n, feat), F32), vmem((lat_n, lon_n, feat), F32), vmem((lat_n, lon_n, feat), F32),
        vmem(mix_coef.shape, F32), vmem(w_in.shape, BF16), vmem(w_out.shape, BF16),
        vmem(patch.shape, jnp.int32), vmem(count.shape, jnp.int32), vmem(pos.shape, jnp.int32),
        vmem(wgt.shape, F32), vmem(rinv.shape, F32),
        vmem((2, lat_n, lon_n, feat), F32), vmem((2 * tok_n, feat), BF16), vmem((4 * (lat_n + lon_n), feat), BF16), vmem((tok_n, hid), F32),
        vmem((tok_n, hid), BF16), vmem((tok_n, feat), BF16), vmem((stations, feat), F32),
        vmem((stations, tok_n), BF16), vmem((tok_n, feat), F32), vmem((tok_n, feat), BF16),
        vmem((lat_n, lon_n, feat), F32),
        vmem((4, 2, 16, feat), BF16), vmem((4, 2, 16, feat), BF16),
        vmem((4, 2, 1, feat), F32), vmem((4, 2, 1, feat), F32),
        vmem((4, 16, feat), BF16), vmem((4, 16, feat), BF16),
        vmem((4, 1, feat), F32), vmem((4, 1, feat), F32),
        vmem((LANES, block_n), F32), vmem((nb, ns, LANES), F32), vmem((nb, ns, LANES), F32),
        vmem((ns, nb, LANES), F32), vmem((ns, nb, LANES), F32),
        vmem((2, LANES), F32), vmem((nb, 2, LANES), F32), vmem((ns, 2, LANES), F32),
        dma((10 + hid // nw,)), dma((2,)), dma((2,)), dma((2,)), dma((2,)), dma((4,)), dma((4,)),
    ]
    sizes = (nb, ns, lat_n, lon_n, feat, hid, slot_n, tap_n, n1, n2, nbk, cw, nw)
    return pl.pallas_call(
        functools.partial(kernel, sizes),
        out_shape=pltpu.VMEM(base_state.shape, F32),
        in_specs=[pl.BlockSpec(memory_space=pl.ANY)] * 11,
        out_specs=pl.BlockSpec(memory_space=pltpu.VMEM),
        scratch_shapes=scratch,
        compiler_params=pltpu.CompilerParams(
            collective_id=0, has_side_effects=True, vmem_limit_bytes=56 * 2**20
        ),
    )(base_state, direction, residual, mix_coef, w_in, w_out, patch, count, pos, wgt, rinv)


def solution(mesh):
    return jax.shard_map(
        functools.partial(shards, mesh.shape["band"], mesh.shape["sector"]),
        mesh=mesh,
        in_specs=(
            P("band", "sector", None),
            P("band", "sector", None),
            P("band", "sector", None),
            P(),
            P(),
            P(),
            P(("band", "sector"), None, None),
            P(("band", "sector"), None),
            P(("band", "sector"), None, None, None),
            P(("band", "sector"), None, None, None),
            P(("band", "sector"), None, None),
        ),
        out_specs=P("band", "sector", None),
        check_vma=False,
    )
```
